256 devices in a mesh: rep: 8 (over y, core), edge: 32 (over z, x).
Axes of the slice: x: 4, y: 4, z: 8, core: 2. Of those that a mesh axis runs over, the one named last changes fastest.
Arguments:
- node_feats: bfloat16 [8, 8192, 128], P('rep', 'edge'), may hold values from -6 to 6
- edge_attr: bfloat16 [8, 65536, 128], P('rep', 'edge'), may hold values from -6 to 6
- edge_src: int32 [8, 65536], P('rep', 'edge'), may hold values from 0 to 8191, as said below
- edge_dst: int32 [8, 65536], P('rep', 'edge'), may hold values from 0 to 8191, as said below
- species: int32 [8, 8192], P('rep'), may hold values from 0 to 2
- orbital_mask: int32 [3, 27], replicated, may hold values 0 or 1
- tile_owner: int32 [8, 65536, 1], P('rep', 'edge'), may hold values from 0 to 31; in each aligned block of 2048 rows (0 to 2047, 2048 to 4095, ..., all dimensions but the last counted through in order) at most 96 rows name the same one
- target_send: bfloat16 [8, 23328, 3072], P('rep', 'edge'), may hold values from -6 to 6
- w_dst: bfloat16 [128, 128], replicated, may hold values from -0.5 to 0.5
- w_src: bfloat16 [128, 128], replicated, may hold values from -0.5 to 0.5
- w_attr: bfloat16 [128, 128], replicated, may hold values from -0.5 to 0.5
- w_mix: bfloat16 [128, 128], replicated, may hold values from -0.5 to 0.5
- w_left: bfloat16 [729, 128], replicated, may hold values from -0.5 to 0.5
- w_right: bfloat16 [729, 128], replicated, may hold values from -0.5 to 0.5
- cg_basis: bfloat16 [729, 729], replicated, may hold values from -0.21875 to 0.21875
Outputs:
- grad_dst: float32 [128, 128], replicated
- grad_src: float32 [128, 128], replicated
- grad_attr: float32 [128, 128], replicated
- grad_mix: float32 [128, 128], replicated
- grad_left: float32 [729, 128], replicated
- grad_right: float32 [729, 128], replicated
- edge_error: float32 [8, 65536], P('rep', 'edge')
The draws below stay inside these ranges and needn't reach their ends.
Inputs may be any that keep to these rules, and one draw needn't show every extreme that they name: `edge_src`: device q of edge holds the edges q * 2048 to (q + 1) * 2048 - 1 and the atoms q * 256 to (q + 1) * 256 - 1 of each structure. An edge's source atom lies in the atoms of its device or of the two devices beside it; on every device both ends of that range occur. `edge_dst`: an edge's target atom lies in the atoms of its own device; on every device both ends of that range occur. `tile_owner`: among the 2048 edges of one device, at most 96 name the same holder.
All inputs are finite; a program needn't handle non-finite values.
Results may differ from the reference program's by a relative error of at most 0.0034.
The reference program's roundings to bfloat16 on the way (of `first`, `second`, `coupled`, `target`, `dpred`, `dmix` and `dpre`) count: a program that leaves them out, or rounds other values in their place, can miss the bound.
Values may be sent and summed in bfloat16 or wider, within the bound.
No kernel may reach another device: no remote copies, remote signals or barrier semaphores. Data moves between devices by JAX's collectives and lax.ppermute only.
A program may use at most 128 MiB of HBM per device.

```python
import math
import jax
import jax.numpy as jnp
import numpy as np
from jax import lax

C = 128
ORB = 27
SPECIES = 3
ATOM_DEV = 256
E_DEV = 2048
ORB2 = 729
CAP = 96
ATOMS = 8192
EDGES = 65536
N_REP = 8
N_EDGE = 32


def atom_ids(key, reach_low, reach_high):
    owner = jnp.arange(N_EDGE * E_DEV, dtype=jnp.int32) // E_DEV
    lowest = jnp.maximum(owner - reach_low, 0) * ATOM_DEV
    highest = jnp.minimum(owner + reach_high, N_EDGE) * ATOM_DEV
    picked = jax.random.randint(key, (N_REP, N_EDGE * E_DEV), lowest[None, :], highest[None, :], dtype=jnp.int32)
    position = jnp.arange(N_EDGE * E_DEV, dtype=jnp.int32) % E_DEV
    picked = jnp.where(position[None, :] == 0, lowest[None, :], picked)
    picked = jnp.where(position[None, :] == 1, highest[None, :] - 1, picked)
    return picked.astype(jnp.int32)


def draw_edge_src(key, part):
    key = jax.random.fold_in(key, 11)
    return atom_ids(key, 1, 2)


def draw_edge_dst(key, part):
    key = jax.random.fold_in(key, 23)
    return atom_ids(key, 0, 1)


def set_ends(entries, stream_key, smallest, top_value):
    longest = entries.shape.index(max(entries.shape))
    spots = []
    for shift in (0, 1):
        where = [jax.random.randint(jax.random.fold_in(stream_key, axis), (), 0, length) for axis, length in enumerate(entries.shape)]
        where[longest] = (where[longest] + shift) % entries.shape[longest]
        spots.append(tuple(where))
    return entries.at[spots[0]].set(smallest).at[spots[1]].set(top_value)


def steps_of(stream_key, extent, pieces, smallest, top_value):
    def one(dim, blocks):
        heights = jax.random.uniform(jax.random.fold_in(jax.random.fold_in(stream_key, 6), dim), (blocks,), jnp.float32, smallest / len(pieces), top_value / len(pieces))
        return jnp.repeat(jnp.exp(heights), extent[dim] // blocks).reshape((-1,) + (1,) * (len(extent) - dim - 1))

    loudness = one(*pieces[0])
    for cut in pieces[1:]:
        loudness = loudness * one(*cut)
    return loudness


def shared_out(own_key, own, number, rows, number_of, top, bound, skew):
    ranking = jax.random.permutation(own_key, number_of)
    crowded, usual = load_shares(number_of, rows * top, bound, skew, True), load_shares(number_of, rows * top, bound, skew, False)
    places = jnp.arange(number_of)

    def named(tallies, rotation):
        used = int((tallies > 0).sum())
        fixed = max(1, used // 4)
        passed = fixed + (places - fixed + rotation * (used - fixed)) % max(1, number_of - fixed)
        return jnp.zeros((number_of,), jnp.int32).at[ranking[jnp.where(places < fixed, places, passed)]].set(jnp.asarray(tallies, jnp.int32))

    tallies = jnp.where(number % 4 == 0, named(crowded, number // 4), named(usual, number - number // 4 - 1))
    mixed = jax.random.permutation(jax.random.fold_in(own, 3), number_of)
    giver, receiver = mixed[0:number_of // 2 * 2:2], mixed[1:number_of // 2 * 2:2]
    margin = jnp.minimum(tallies[giver] - 1, bound - tallies[receiver]) // 2
    margin = jnp.where((giver == ranking[0]) | (receiver == ranking[0]) | (tallies[receiver] == 0), 0, jnp.maximum(margin, 0))
    passed = jax.random.randint(jax.random.fold_in(own, 4), (number_of // 2,), 0, 1 << 20) % (margin + 1)
    tallies = tallies.at[giver].add(-passed).at[receiver].add(passed)
    members = jnp.searchsorted(jnp.cumsum(tallies), jnp.arange(rows * top), side="right").astype(jnp.int32)
    grid = members.reshape(top, rows).T
    grid = grid[jax.random.permutation(jax.random.fold_in(own, 1), rows)]
    rotation = jax.random.randint(jax.random.fold_in(own, 2), (rows, 1), 0, top)
    return jnp.take_along_axis(grid, (jnp.arange(top)[None, :] + rotation) % top, axis=1)


def load_shares(amount, total, bound, slope, full):
    loads = [(1 << 20) // math.isqrt(standing ** slope) + 1 for standing in range(1, amount + 1)]
    largest = bound if full else min(bound, max(-(-total // amount), total * loads[0] // sum(loads)))
    least = 1 if total - largest >= amount - 1 else 0
    holding, rest = [largest] + [least] * (amount - 1), total - largest - least * (amount - 1)
    while rest > 0:
        free = [i for i in range(1, amount) if holding[i] < largest] or [i for i in range(1, amount) if holding[i] < bound]
        mass, remaining = sum([loads[i] for i in free]), rest
        for i in free:
            extra = min(bound - holding[i], max(1, remaining * loads[i] // mass), rest)
            holding[i] = holding[i] + extra
            rest = rest - extra
    return np.array(holding)


def gaussian(own_key, shape, deviation, bound, split=(), held_as=jnp.bfloat16):
    drawn = deviation * jax.random.normal(own_key, shape, jnp.float32)
    if split:
        drawn = drawn * steps_of(own_key, shape, split, -0.22, 0.18)
    return jnp.clip(drawn, -bound, bound).astype(held_as)


def setup_inputs(seed: int = 0) -> dict:
    splits = jax.random.split(jax.random.key(seed), 16)
    node_feats = gaussian(splits[0], (N_REP, ATOMS, C), 1.0, 6.0, ((0, 8), (1, 32)))
    edge_attr = gaussian(splits[1], (N_REP, EDGES, C), 1.0, 6.0, ((0, 8), (1, 32)))
    edge_src = draw_edge_src(jax.random.fold_in(splits[15], 71), 0)
    edge_dst = draw_edge_dst(jax.random.fold_in(splits[15], 71), 0)
    species = set_ends(jax.random.randint(splits[4], (N_REP, ATOMS), 0, SPECIES), jax.random.fold_in(splits[4], 1), 0, SPECIES - 1).astype(jnp.int32)
    orbital_mask = set_ends((jax.random.randint(splits[5], (SPECIES, ORB), 0, 4) < 3).astype(jnp.int32), jax.random.fold_in(splits[5], 1), 0, 1)
    tile_owner_keys = jax.random.split(jax.random.fold_in(splits[6], 1), N_REP * EDGES // E_DEV)
    tile_owner_turns = jax.random.permutation(jax.random.fold_in(splits[6], 3), N_REP * EDGES // E_DEV)
    tile_owner = jax.vmap(lambda own, number: shared_out(jax.random.fold_in(splits[6], 2), own, number, E_DEV, N_EDGE, 1, CAP, 2))(tile_owner_keys, tile_owner_turns).reshape((N_REP, EDGES, 1))
    target_send = gaussian(splits[7], (N_REP, N_EDGE * ORB2, N_EDGE * CAP), 1.0, 6.0, ((0, 8), (1, 32)))
    w_dst = gaussian(splits[8], (C, C), C ** -0.5, 0.5)
    w_src = gaussian(splits[9], (C, C), C ** -0.5, 0.5)
    w_attr = gaussian(splits[10], (C, C), C ** -0.5, 0.5)
    w_mix = gaussian(splits[11], (C, C), C ** -0.5, 0.5)
    w_left = gaussian(splits[12], (ORB2, C), C ** -0.5, 0.5)
    w_right = gaussian(splits[13], (ORB2, C), C ** -0.5, 0.5)
    cg_basis = gaussian(splits[14], (ORB2, ORB2), ORB2 ** -0.5, 0.21875)
    return {"node_feats": node_feats, "edge_attr": edge_attr, "edge_src": edge_src, "edge_dst": edge_dst, "species": species, "orbital_mask": orbital_mask, "tile_owner": tile_owner, "target_send": target_send, "w_dst": w_dst, "w_src": w_src, "w_attr": w_attr, "w_mix": w_mix, "w_left": w_left, "w_right": w_right, "cg_basis": cg_basis}


def silu_slope(value):
    sigma = jax.nn.sigmoid(value)
    return sigma * (1.0 + value * (1.0 - sigma))


def edge_block(feat_dst, feat_src, attr, spec_dst, spec_src, target, w_dst, w_src, w_attr, w_mix, w_left, w_right, cg_basis, orbital_mask):
    pre = jnp.dot(feat_dst, w_dst, preferred_element_type=jnp.float32)
    pre = pre + jnp.dot(feat_src, w_src, preferred_element_type=jnp.float32)
    pre = pre + jnp.dot(attr, w_attr, preferred_element_type=jnp.float32)
    first = jax.nn.silu(pre).astype(jnp.bfloat16)
    mixpre = jnp.dot(first, w_mix, preferred_element_type=jnp.float32)
    second = (first.astype(jnp.float32) + jax.nn.silu(mixpre)).astype(jnp.bfloat16)
    contract_c = (((1,), (1,)), ((), ()))
    left_t = lax.dot_general(w_left, second, contract_c, preferred_element_type=jnp.float32)
    right_t = lax.dot_general(w_right, second, contract_c, preferred_element_type=jnp.float32)
    coupled = (left_t * right_t).astype(jnp.bfloat16)
    predicted = lax.dot_general(cg_basis, coupled, (((0,), (0,)), ((), ())), preferred_element_type=jnp.float32)
    kinds = orbital_mask.shape[0]
    orbs = orbital_mask.shape[1]
    table = orbital_mask.astype(jnp.float32).T
    onehot_dst = (jnp.arange(kinds, dtype=jnp.int32)[:, None] == spec_dst[None, :]).astype(jnp.float32)
    onehot_src = (jnp.arange(kinds, dtype=jnp.int32)[:, None] == spec_src[None, :]).astype(jnp.float32)
    rows_dst = jnp.dot(table, onehot_dst)
    rows_src = jnp.dot(table, onehot_src)
    mask = (rows_dst[:, None, :] * rows_src[None, :, :]).reshape(orbs * orbs, -1)
    resid = mask * (predicted - target.astype(jnp.float32))
    errors = jnp.sum(resid * resid, axis=0) / (orbs * orbs)
    dpred = (resid / (orbs * orbs)).astype(jnp.bfloat16)
    dcoupled = jnp.dot(cg_basis, dpred, preferred_element_type=jnp.float32)
    dleft = (dcoupled * right_t).astype(jnp.bfloat16)
    dright = (dcoupled * left_t).astype(jnp.bfloat16)
    grad_left = jnp.dot(dleft, second, preferred_element_type=jnp.float32)
    grad_right = jnp.dot(dright, second, preferred_element_type=jnp.float32)
    contract_rows = (((0,), (0,)), ((), ()))
    dsecond = lax.dot_general(dleft, w_left, contract_rows, preferred_element_type=jnp.float32)
    dsecond = dsecond + lax.dot_general(dright, w_right, contract_rows, preferred_element_type=jnp.float32)
    dmix = (dsecond * silu_slope(mixpre)).astype(jnp.bfloat16)
    grad_mix = lax.dot_general(first, dmix, contract_rows, preferred_element_type=jnp.float32)
    dfirst = dsecond + lax.dot_general(dmix, w_mix, contract_c, preferred_element_type=jnp.float32)
    dpre = (dfirst * silu_slope(pre)).astype(jnp.bfloat16)
    grad_dst = lax.dot_general(feat_dst, dpre, contract_rows, preferred_element_type=jnp.float32)
    grad_src = lax.dot_general(feat_src, dpre, contract_rows, preferred_element_type=jnp.float32)
    grad_attr = lax.dot_general(attr, dpre, contract_rows, preferred_element_type=jnp.float32)
    return (grad_dst, grad_src, grad_attr, grad_mix, grad_left, grad_right), errors


def reference(node_feats, edge_attr, edge_src, edge_dst, species, orbital_mask, tile_owner, target_send, w_dst, w_src, w_attr, w_mix, w_left, w_right, cg_basis):
    holders = target_send.reshape(N_REP, N_EDGE, ORB2, N_EDGE * CAP)

    def one_block(running, block_id):
        replica = block_id // N_EDGE
        device = block_id % N_EDGE
        start = (device * E_DEV).astype(jnp.int32)
        src_ids = lax.dynamic_slice_in_dim(edge_src[replica], start, E_DEV)
        dst_ids = lax.dynamic_slice_in_dim(edge_dst[replica], start, E_DEV)
        attr = lax.dynamic_slice_in_dim(edge_attr[replica], start, E_DEV, 0)
        holder = lax.dynamic_slice_in_dim(tile_owner[replica][:, 0], start, E_DEV)
        feats = node_feats[replica]
        feat_src = jnp.take(feats, src_ids, axis=0)
        feat_dst = jnp.take(feats, dst_ids, axis=0)
        kinds = species[replica]
        spec_src = jnp.take(kinds, src_ids)
        spec_dst = jnp.take(kinds, dst_ids)
        onehot = (holder[:, None] == jnp.arange(N_EDGE, dtype=jnp.int32)[None, :]).astype(jnp.int32)
        before = jnp.cumsum(onehot, axis=0) - onehot
        rank = jnp.sum(before * onehot, axis=1).astype(jnp.int32)
        columns = (device * CAP + rank).astype(jnp.int32)
        stored = holders[replica]
        target = stored[holder[None, :], jnp.arange(ORB2, dtype=jnp.int32)[:, None], columns[None, :]]
        grads, errors = edge_block(feat_dst, feat_src, attr, spec_dst, spec_src, target, w_dst, w_src, w_attr, w_mix, w_left, w_right, cg_basis, orbital_mask)
        running = tuple(total + part for total, part in zip(running, grads))
        return running, errors

    zeros_square = jnp.zeros((C, C), jnp.float32)
    zeros_wide = jnp.zeros((ORB2, C), jnp.float32)
    start_sums = (zeros_square, zeros_square, zeros_square, zeros_square, zeros_wide, zeros_wide)
    running, errors = lax.scan(one_block, start_sums, jnp.arange(N_REP * N_EDGE, dtype=jnp.int32))
    return (running[0], running[1], running[2], running[3], running[4], running[5], errors.reshape(N_REP, EDGES))
```

```python
import jax
import jax.numpy as jnp
import numpy as np
from jax import lax
from jax.experimental import pallas as pl
from jax.experimental.pallas import tpu as pltpu
from jax.sharding import PartitionSpec as P

F32 = jnp.float32
BF16 = jnp.bfloat16
GROUP = 8
TAIL = 16
LANES = 128
CHUNK = 256
MIB = 1 << 20


def ring(count, shift):
    return [(i, (i + shift) % count) for i in range(count)]


def matmul(a, b):
    return jnp.dot(a, b, preferred_element_type=F32)


def matmul_nt(a, b):
    return lax.dot_general(a, b, (((1,), (1,)), ((), ())), preferred_element_type=F32)


def matmul_tn(a, b):
    return lax.dot_general(a, b, (((0,), (0,)), ((), ())), preferred_element_type=F32)


def indicator(condition):
    return jnp.where(condition, 1.0, 0.0).astype(BF16)


def slope(value, sigma):
    return sigma * (1.0 + value * (1.0 - sigma))


def slot_onehot(out, holder, rank, base, capacity):
    edges = holder.shape[1]
    place = lax.broadcasted_iota(jnp.int32, (capacity, edges), 0)
    for p in range(GROUP):
        mine = jnp.where(holder == base + p, rank, -1)
        out[p * capacity : (p + 1) * capacity, :] = indicator(place == mine)


def edge_kernel(
    pos_ref,
    dst_ref,
    src_ref,
    holder_ref,
    spec_lo,
    spec_mid,
    spec_hi,
    node_lo,
    node_mid,
    node_hi,
    attr_ref,
    wdst_t,
    wsrc_t,
    wattr_t,
    wmix_t,
    out_ref,
    rank_ref,
    xdst_ref,
    xsrc_ref,
    first_ref,
    pre_ref,
    mixpre_ref,
    second,
    onehot,
    tags,
):
    step = pl.program_id(0)
    edges = dst_ref.shape[1]
    devices = tags.shape[0] // 2
    capacity = out_ref.shape[1] - TAIL
    atoms = node_mid.shape[0]
    holder = holder_ref[...]

    @pl.when(step == 0)
    def _():
        offset = pos_ref[0] * atoms
        same = lax.broadcasted_iota(jnp.int32, (devices, edges), 0) == holder
        named = jnp.where(same, 1.0, 0.0)
        named_bf = named.astype(BF16)
        rows = lax.broadcasted_iota(jnp.int32, (CHUNK, CHUNK), 0)
        cols = lax.broadcasted_iota(jnp.int32, (CHUNK, CHUNK), 1)
        earlier = indicator(rows < cols)
        carry = jnp.zeros((devices, 1), F32)
        for c in range(edges // CHUNK):
            part = slice(c * CHUNK, (c + 1) * CHUNK)
            before = matmul(named_bf[:, part], earlier) + carry
            carry = carry + jnp.sum(named[:, part], axis=1, keepdims=True)
            rank_ref[:, part] = jnp.sum(
                before * named[:, part], axis=0, keepdims=True
            ).astype(jnp.int32)
        rank = rank_ref[...]

        def table_of(nodes, spec):
            kinds = jnp.broadcast_to((spec[...] + 1).astype(F32), (TAIL, atoms)).astype(BF16)
            return jnp.concatenate([nodes[...].T, kinds], axis=0)

        table_mid = table_of(node_mid, spec_mid)
        table = jnp.concatenate(
            [table_of(node_lo, spec_lo), table_mid, table_of(node_hi, spec_hi)], axis=1
        )
        channels = node_mid.shape[1]
        ids = lax.broadcasted_iota(jnp.int32, (atoms, edges), 0)
        from_dst = matmul(table_mid, indicator(ids == dst_ref[...] - offset))
        ids = lax.broadcasted_iota(jnp.int32, (3 * atoms, edges), 0)
        from_src = matmul(table, indicator(ids == src_ref[...] - (offset - atoms)))
        xdst = from_dst[:channels].astype(BF16)
        xsrc = from_src[:channels].astype(BF16)
        xdst_ref[...] = xdst
        xsrc_ref[...] = xsrc
        pre = matmul(wdst_t[...], xdst) + matmul(wsrc_t[...], xsrc)
        pre = pre + matmul_nt(wattr_t[...], attr_ref[...])
        pre_ref[...] = pre
        first = (pre * jax.nn.sigmoid(pre)).astype(BF16)
        first_ref[...] = first
        mixpre = matmul(wmix_t[...], first)
        mixpre_ref[...] = mixpre
        second[...] = (first.astype(F32) + mixpre * jax.nn.sigmoid(mixpre)).astype(BF16)
        tagged = jnp.concatenate(
            [named * from_dst[channels : channels + 1], named * from_src[channels : channels + 1]],
            axis=0,
        ).astype(BF16)
        at_rank = indicator(lax.broadcasted_iota(jnp.int32, (LANES, edges), 0) == rank)
        tags[...] = matmul_nt(tagged, at_rank)

    slot_onehot(onehot, holder, rank_ref[...], step * GROUP, capacity)
    moved = matmul_nt(onehot[...], second[...]).astype(BF16)
    line = lax.broadcasted_iota(jnp.int32, (TAIL, LANES), 0)
    for p in range(GROUP):
        out_ref[p, :capacity, :] = moved[p * capacity : (p + 1) * capacity]
        tag_dst = tags[pl.ds(step * GROUP + p, 1), :]
        tag_src = tags[pl.ds(devices + step * GROUP + p, 1), :]
        tail = jnp.where(line == 0, tag_dst, jnp.where(line == 1, tag_src, 0.0))
        out_ref[p, capacity:, :] = tail.astype(BF16)


def holder_kernel(
    recv_ref,
    target_ref,
    wlr_ref,
    wlr_t,
    cg_ref,
    cg_t,
    pairs_ref,
    place_ref,
    back_ref,
    grad_ref,
    dlr,
):
    step = pl.program_id(0)
    capacity = recv_ref.shape[1] - TAIL
    width = GROUP * capacity
    channels = recv_ref.shape[2]
    rows = cg_ref.shape[0]
    orb2 = target_ref.shape[1]
    kinds = 3
    second = recv_ref[:, :capacity, :].reshape(width, channels)
    line = lax.broadcasted_iota(jnp.int32, (GROUP * TAIL, width), 0)
    start = place_ref[0:1, :]
    spread = indicator(lax.broadcasted_iota(jnp.int32, (LANES, width), 0) == place_ref[1:2, :])
    tails = recv_ref[:, capacity:, :].reshape(GROUP * TAIL, LANES)
    tags = matmul(tails, spread)
    tag_dst = jnp.sum(jnp.where(line == start, tags, 0.0), axis=0, keepdims=True)
    tag_src = jnp.sum(jnp.where(line == start + 1, tags, 0.0), axis=0, keepdims=True)
    code = jnp.where(tag_dst > 0.5, (tag_dst - 1.0) * kinds + (tag_src - 1.0), -1.0)
    code = code.astype(jnp.int32)
    pair_line = lax.broadcasted_iota(jnp.int32, (pairs_ref.shape[1], width), 0)
    pair = indicator(pair_line == code)
    errors = []
    for n in range(width // CHUNK):
        part = slice(n * CHUNK, (n + 1) * CHUNK)
        both = matmul_nt(wlr_ref[...], second[part])
        left = both[:rows]
        right = both[rows:]
        predicted = matmul(cg_t[...], (left * right).astype(BF16))
        mask = matmul(pairs_ref[...], pair[:, part])
        goal = target_ref[0, :, part].astype(F32)
        goal = jnp.concatenate([goal, jnp.zeros((rows - orb2, CHUNK), F32)], axis=0)
        resid = mask * (predicted - goal)
        errors.append(jnp.sum(resid * resid, axis=0, keepdims=True) / orb2)
        dpred = (resid / orb2).astype(BF16)
        dcoupled = matmul(cg_ref[...], dpred)
        dlr[:rows, part] = (dcoupled * right).astype(BF16)
        dlr[rows:, part] = (dcoupled * left).astype(BF16)
    dsecond = matmul(wlr_t[...], dlr[...])
    moved = dsecond.T.astype(BF16)
    for q in range(GROUP):
        back_ref[q, :capacity, :] = moved[q * capacity : (q + 1) * capacity]
    error = jnp.concatenate(errors, axis=1)
    high = error.astype(BF16).astype(F32)
    middle = (error - high).astype(BF16).astype(F32)
    low = error - high - middle
    packed = jnp.where(
        line == start,
        high,
        jnp.where(line == start + 1, middle, jnp.where(line == start + 2, low, 0.0)),
    ).astype(BF16)
    spelled = matmul_nt(packed, spread).astype(BF16)
    for q in range(GROUP):
        back_ref[q, capacity:, :] = spelled[q * TAIL : (q + 1) * TAIL]
    grad = matmul(dlr[...], second)

    @pl.when(step == 0)
    def _():
        grad_ref[...] = grad

    @pl.when(step > 0)
    def _():
        grad_ref[...] += grad


def finish_kernel(
    back_ref,
    holder_ref,
    rank_ref,
    xdst_ref,
    xsrc_ref,
    attr_ref,
    first_ref,
    pre_ref,
    mixpre_ref,
    wmix,
    grad_ref,
    error_ref,
    onehot,
    dsecond,
    found,
):
    step = pl.program_id(0)
    capacity = back_ref.shape[1] - TAIL
    edges = holder_ref.shape[1]
    channels = back_ref.shape[2]
    holder = holder_ref[...]
    rank = rank_ref[...]

    @pl.when(step == 0)
    def _():
        dsecond[...] = jnp.zeros_like(dsecond)
        found[...] = jnp.zeros_like(found)

    slot_onehot(onehot, holder, rank, step * GROUP, capacity)
    rows = back_ref[:, :capacity, :].reshape(GROUP * capacity, channels)
    dsecond[...] += matmul_tn(rows, onehot[...])
    line = lax.broadcasted_iota(jnp.int32, (GROUP * TAIL, edges), 0)
    low = (holder - step * GROUP) * TAIL
    at_holder = indicator(jnp.logical_and(line >= low, line < low + TAIL))
    tails = back_ref[:, capacity:, :].reshape(GROUP * TAIL, LANES)
    found[...] += matmul_tn(tails, at_holder)

    @pl.when(step == pl.num_programs(0) - 1)
    def _():
        place = lax.broadcasted_iota(jnp.int32, found.shape, 0)
        error_ref[...] = jnp.sum(
            jnp.where(place == rank, found[...], 0.0), axis=0, keepdims=True
        )
        dsec = dsecond[...]
        mixpre = mixpre_ref[...]
        dmix = (dsec * slope(mixpre, jax.nn.sigmoid(mixpre))).astype(BF16)
        dfirst = dsec + matmul(wmix[...], dmix)
        pre = pre_ref[...]
        dpre = (dfirst * slope(pre, jax.nn.sigmoid(pre))).astype(BF16)
        grad_ref[0:channels] = matmul_nt(xdst_ref[...], dpre)
        grad_ref[channels : 2 * channels] = matmul_nt(xsrc_ref[...], dpre)
        grad_ref[2 * channels : 3 * channels] = matmul(dpre, attr_ref[...]).T
        grad_ref[3 * channels : 4 * channels] = matmul_nt(first_ref[...], dmix)


def exchange(array, axis, groups):
    return lax.all_to_all(
        array, axis, split_axis=0, concat_axis=0, tiled=True, axis_index_groups=groups
    )


def sum_everywhere(part, wide, narrow, deep):
    half = part.shape[0] // 2
    core = lax.rem(lax.axis_index("rep"), 2)
    swap = [(i, i ^ 1) for i in range(wide * 2)]
    keep = lax.dynamic_slice_in_dim(part, core * half, half, 0)
    give = lax.dynamic_slice_in_dim(part, (1 - core) * half, half, 0)
    part = keep + lax.ppermute(give, "rep", swap)
    edge = narrow * deep
    plane = [
        [(y * 2 + c) * edge + z * narrow + x for y in range(wide) for x in range(narrow)]
        for c in range(2)
        for z in range(deep)
    ]
    column = [[z * narrow + x for z in range(deep)] for x in range(narrow)]
    peers = wide * narrow
    got = exchange(part, ("rep", "edge"), plane)
    part = jnp.sum(got.reshape(peers, half // peers, -1), axis=0)
    got = exchange(jnp.tile(part, (deep, 1)), "edge", column)
    part = jnp.sum(got.reshape(deep, half // peers, -1), axis=0)
    part = exchange(jnp.tile(part, (peers, 1)), ("rep", "edge"), plane)
    other = lax.ppermute(part, "rep", swap)
    low = jnp.where(core == 0, part, other)
    high = jnp.where(core == 0, other, part)
    return jnp.concatenate([low, high], axis=0)


def local(
    node_feats,
    edge_attr,
    edge_src,
    edge_dst,
    species,
    orbital_mask,
    tile_owner,
    target_send,
    w_dst,
    w_src,
    w_attr,
    w_mix,
    w_left,
    w_right,
    cg_basis,
):
    atoms, channels = node_feats.shape[1:]
    edges = edge_attr.shape[1]
    orb2, columns = target_send.shape[1:]
    devices = lax.axis_size("edge")
    capacity = columns // devices
    steps = devices // GROUP
    block = capacity + TAIL
    position = lax.axis_index("edge")
    rows = -(-orb2 // 32) * 32
    nodes = node_feats[0]
    node_lo = lax.ppermute(nodes, "edge", ring(devices, 1))
    node_hi = lax.ppermute(nodes, "edge", ring(devices, -1))
    holder = tile_owner.reshape(1, edges)
    attr = edge_attr[0]

    def whole(shape):
        return pl.BlockSpec(shape, lambda *_: (0,) * len(shape))

    def kinds_of(shift):
        return pl.BlockSpec(
            (1, atoms), lambda i, pos: (0, jnp.clip(pos[0] + shift, 0, devices - 1))
        )

    square = whole((channels, channels))
    line = whole((1, edges))
    wide = whole((channels, edges))
    sent, rank, xdst, xsrc, first, pre, mixpre = pl.pallas_call(
        edge_kernel,
        out_shape=(
            jax.ShapeDtypeStruct((devices, block, channels), BF16),
            jax.ShapeDtypeStruct((1, edges), jnp.int32),
            jax.ShapeDtypeStruct((channels, edges), BF16),
            jax.ShapeDtypeStruct((channels, edges), BF16),
            jax.ShapeDtypeStruct((channels, edges), BF16),
            jax.ShapeDtypeStruct((channels, edges), F32),
            jax.ShapeDtypeStruct((channels, edges), F32),
        ),
        grid_spec=pltpu.PrefetchScalarGridSpec(
            num_scalar_prefetch=1,
            grid=(steps,),
            in_specs=[
                line,
                line,
                line,
                kinds_of(-1),
                kinds_of(0),
                kinds_of(1),
                whole((atoms, channels)),
                whole((atoms, channels)),
                whole((atoms, channels)),
                whole((edges, channels)),
                square,
                square,
                square,
                square,
            ],
            out_specs=[
                pl.BlockSpec((GROUP, block, channels), lambda i, pos: (i, 0, 0)),
                line,
                wide,
                wide,
                wide,
                wide,
                wide,
            ],
            scratch_shapes=[
                pltpu.VMEM((channels, edges), BF16),
                pltpu.VMEM((GROUP * capacity, edges), BF16),
                pltpu.VMEM((2 * devices, LANES), F32),
            ],
        ),
        compiler_params=pltpu.CompilerParams(vmem_limit_bytes=48 * MIB),
    )(
        position.astype(jnp.int32)[None],
        edge_dst,
        edge_src,
        holder,
        species,
        species,
        species,
        node_lo,
        nodes,
        node_hi,
        attr,
        w_dst.T,
        w_src.T,
        w_attr.T,
        w_mix.T,
    )

    received = lax.all_to_all(sent, "edge", split_axis=0, concat_axis=0, tiled=True)

    pad = ((0, rows - orb2), (0, 0))
    wlr = jnp.concatenate([jnp.pad(w_left, pad), jnp.pad(w_right, pad)], axis=0)
    cg = jnp.pad(cg_basis, ((0, rows - orb2), (0, rows - orb2)))
    carried = orbital_mask.astype(F32)
    pairs = (carried[:, None, :, None] * carried[None, :, None, :]).reshape(-1, orb2).T
    pairs = jnp.pad(pairs, ((0, rows - orb2), (0, TAIL - pairs.shape[1]))).astype(BF16)
    slots = np.arange(GROUP * capacity)
    places = jnp.asarray(
        np.stack([slots // capacity * TAIL, slots % capacity]).astype(np.int32)
    )
    back, grad_wide = pl.pallas_call(
        holder_kernel,
        out_shape=(
            jax.ShapeDtypeStruct((devices, block, channels), BF16),
            jax.ShapeDtypeStruct((2 * rows, channels), F32),
        ),
        grid=(steps,),
        in_specs=[
            pl.BlockSpec((GROUP, block, channels), lambda i: (i, 0, 0)),
            pl.BlockSpec((1, orb2, GROUP * capacity), lambda i: (0, 0, i)),
            whole(wlr.shape),
            whole(wlr.shape[::-1]),
            whole(cg.shape),
            whole(cg.shape),
            whole(pairs.shape),
            whole(places.shape),
        ],
        out_specs=[
            pl.BlockSpec((GROUP, block, channels), lambda i: (i, 0, 0)),
            whole((2 * rows, channels)),
        ],
        scratch_shapes=[pltpu.VMEM((2 * rows, GROUP * capacity), BF16)],
        compiler_params=pltpu.CompilerParams(vmem_limit_bytes=56 * MIB),
    )(received, target_send, wlr, wlr.T, cg, cg.T, pairs, places)

    returned = lax.all_to_all(back, "edge", split_axis=0, concat_axis=0, tiled=True)

    grad_small, errors = pl.pallas_call(
        finish_kernel,
        out_shape=(
            jax.ShapeDtypeStruct((4 * channels, channels), F32),
            jax.ShapeDtypeStruct((1, edges), F32),
        ),
        grid=(steps,),
        in_specs=[
            pl.BlockSpec((GROUP, block, channels), lambda i: (i, 0, 0)),
            line,
            line,
            wide,
            wide,
            whole((edges, channels)),
            wide,
            wide,
            wide,
            square,
        ],
        out_specs=[whole((4 * channels, channels)), line],
        scratch_shapes=[
            pltpu.VMEM((GROUP * capacity, edges), BF16),
            pltpu.VMEM((channels, edges), F32),
            pltpu.VMEM((LANES, edges), F32),
        ],
        compiler_params=pltpu.CompilerParams(vmem_limit_bytes=48 * MIB),
    )(returned, holder, rank, xdst, xsrc, attr, first, pre, mixpre, w_mix)

    used = 4 * channels + 2 * rows
    unit = 256 * 8
    total = -(-used // unit) * unit
    grads = jnp.concatenate(
        [grad_small, grad_wide, jnp.zeros((total - used, channels), F32)], axis=0
    )
    grads = sum_everywhere(grads, 4, 4, 8)
    outs = [grads[i * channels : (i + 1) * channels] for i in range(4)]
    outs += [grads[4 * channels + i * rows :][:orb2] for i in range(2)]
    return (*outs, errors)


def solution(mesh):
    return jax.shard_map(
        local,
        mesh=mesh,
        in_specs=(
            P("rep", "edge", None),
            P("rep", "edge", None),
            P("rep", "edge"),
            P("rep", "edge"),
            P("rep", None),
            P(),
            P("rep", "edge", None),
            P("rep", "edge", None),
            P(),
            P(),
            P(),
            P(),
            P(),
            P(),
            P(),
        ),
        out_specs=(P(), P(), P(), P(), P(), P(), P("rep", "edge")),
        check_vma=False,
    )
```

```python
import functools

import jax
import jax.numpy as jnp
import numpy as np
from jax import lax
from jax.experimental import pallas as pl
from jax.experimental.pallas import tpu as pltpu
from jax.sharding import PartitionSpec as P

F32 = jnp.float32
BF16 = jnp.bfloat16
GROUP = 16
TAIL = 16
LANES = 128
CHUNK = 256
VMEM = 60 << 20


def ring(count, shift):
    return [(i, (i + shift) % count) for i in range(count)]


def matmul(a, b):
    return jnp.dot(a, b, preferred_element_type=F32)


def matmul_nt(a, b):
    return lax.dot_general(a, b, (((1,), (1,)), ((), ())), preferred_element_type=F32)


def matmul_tn(a, b):
    return lax.dot_general(a, b, (((0,), (0,)), ((), ())), preferred_element_type=F32)


def indicator(condition):
    return jnp.where(condition, 1.0, 0.0).astype(BF16)


def slope(value, sigma):
    return sigma * (1.0 + value * (1.0 - sigma))


def slot_onehot(out, holder, rank, base, capacity):
    edges = holder.shape[1]
    place = lax.broadcasted_iota(jnp.int32, (capacity, edges), 0)
    for p in range(GROUP):
        mine = jnp.where(holder == base + p, rank, -1)
        out[p * capacity : (p + 1) * capacity, :] = indicator(place == mine)


def edge_kernel(
    pos_ref,
    dst_ref,
    src_ref,
    holder_ref,
    spec_lo,
    spec_mid,
    spec_hi,
    node_lo,
    node_mid,
    node_hi,
    attr_ref,
    w_dst,
    w_src,
    w_attr,
    w_mix,
    out_ref,
    rank_ref,
    xdst_ref,
    xsrc_ref,
    first_ref,
    pre_ref,
    mixpre_ref,
    second_ref,
    onehot,
    tags,
):
    step = pl.program_id(0)
    edges = dst_ref.shape[1]
    devices = tags.shape[0] // 2
    capacity = out_ref.shape[1] - TAIL
    atoms = node_mid.shape[0]
    holder = holder_ref[...]

    @pl.when(step == 0)
    def _():
        offset = pos_ref[0] * atoms
        same = lax.broadcasted_iota(jnp.int32, (devices, edges), 0) == holder
        named = jnp.where(same, 1.0, 0.0)
        named_bf = named.astype(BF16)
        rows = lax.broadcasted_iota(jnp.int32, (CHUNK, CHUNK), 0)
        cols = lax.broadcasted_iota(jnp.int32, (CHUNK, CHUNK), 1)
        earlier = indicator(rows < cols)
        carry = jnp.zeros((devices, 1), F32)
        for c in range(edges // CHUNK):
            part = slice(c * CHUNK, (c + 1) * CHUNK)
            before = matmul(named_bf[:, part], earlier) + carry
            carry = carry + jnp.sum(named[:, part], axis=1, keepdims=True)
            rank_ref[:, part] = jnp.sum(
                before * named[:, part], axis=0, keepdims=True
            ).astype(jnp.int32)
        rank = rank_ref[...]

        def table_of(nodes, spec):
            kinds = jnp.broadcast_to((spec[...] + 1).astype(F32), (TAIL, atoms)).astype(BF16)
            return jnp.concatenate([nodes[...].T, kinds], axis=0)

        table_mid = table_of(node_mid, spec_mid)
        table = jnp.concatenate(
            [table_of(node_lo, spec_lo), table_mid, table_of(node_hi, spec_hi)], axis=1
        )
        channels = node_mid.shape[1]
        ids = lax.broadcasted_iota(jnp.int32, (atoms, edges), 0)
        from_dst = matmul(table_mid, indicator(ids == dst_ref[...] - offset))
        ids = lax.broadcasted_iota(jnp.int32, (3 * atoms, edges), 0)
        from_src = matmul(table, indicator(ids == src_ref[...] - (offset - atoms)))
        xdst = from_dst[:channels].astype(BF16)
        xsrc = from_src[:channels].astype(BF16)
        xdst_ref[...] = xdst
        xsrc_ref[...] = xsrc
        pre = matmul(w_dst[...].T, xdst) + matmul(w_src[...].T, xsrc)
        pre = pre + matmul_nt(w_attr[...].T, attr_ref[...])
        pre_ref[...] = pre
        first = (pre * jax.nn.sigmoid(pre)).astype(BF16)
        first_ref[...] = first
        mixpre = matmul(w_mix[...].T, first)
        mixpre_ref[...] = mixpre
        second_ref[...] = (first.astype(F32) + mixpre * jax.nn.sigmoid(mixpre)).astype(BF16)
        tagged = jnp.concatenate(
            [named * from_dst[channels : channels + 1], named * from_src[channels : channels + 1]],
            axis=0,
        ).astype(BF16)
        at_rank = indicator(lax.broadcasted_iota(jnp.int32, (LANES, edges), 0) == rank)
        tags[...] = matmul_nt(tagged, at_rank)

    slot_onehot(onehot, holder, rank_ref[...], step * GROUP, capacity)
    moved = matmul_nt(onehot[...], second_ref[...]).astype(BF16)
    line = lax.broadcasted_iota(jnp.int32, (TAIL, LANES), 0)
    for p in range(GROUP):
        out_ref[p, :capacity, :] = moved[p * capacity : (p + 1) * capacity]
        tag_dst = tags[pl.ds(step * GROUP + p, 1), :]
        tag_src = tags[pl.ds(devices + step * GROUP + p, 1), :]
        tail = jnp.where(line == 0, tag_dst, jnp.where(line == 1, tag_src, 0.0))
        out_ref[p, capacity:, :] = tail.astype(BF16)


def later_kernel(holder_ref, rank_ref, second_ref, out_ref, onehot):
    capacity = out_ref.shape[1]
    base = pl.program_id(0) * GROUP
    slot_onehot(onehot, holder_ref[...], rank_ref[...] - capacity, base, capacity)
    moved = matmul_nt(onehot[...], second_ref[...]).astype(BF16)
    for p in range(GROUP):
        out_ref[p] = moved[p * capacity : (p + 1) * capacity]


def prepare_kernel(
    target_ref,
    moves_ref,
    cg_ref,
    wleft_ref,
    wright_ref,
    mask_ref,
    pick_a,
    pick_b,
    pick_dst,
    pick_src,
    early_ref,
    later_ref,
    cg_out,
    cg_t,
    wlr_out,
    pairs_ref,
):
    rows = early_ref.shape[0]
    half = early_ref.shape[1]
    orb2 = target_ref.shape[1]
    width = 2 * half

    def pad_rows(array):
        empty = jnp.zeros((rows - orb2, array.shape[1]), array.dtype)
        return jnp.concatenate([array, empty], axis=0)

    moves = indicator(lax.broadcasted_iota(jnp.int32, (width, width), 0) == moves_ref[...])
    moved = pad_rows(matmul(target_ref[0], moves)).astype(BF16)
    early_ref[...] = moved[:, :half]
    later_ref[...] = moved[:, half:]

    @pl.when(pl.program_id(0) == 0)
    def _():
        tall = pad_rows(cg_ref[...].astype(F32))
        across = jnp.concatenate([tall, jnp.zeros((rows, rows - orb2), F32)], axis=1)
        cg_out[...] = across.astype(BF16)
        cg_t[...] = across.T.astype(BF16)
        left = pad_rows(wleft_ref[...].astype(F32))
        right = pad_rows(wright_ref[...].astype(F32))
        both = jnp.concatenate([left, right], axis=0)
        wlr_out[...] = both.astype(BF16)
        carried = mask_ref[...].astype(F32).astype(BF16)
        dst = matmul_tn(carried, pick_dst[...]).astype(BF16)
        src = matmul_tn(carried, pick_src[...]).astype(BF16)
        pairs_ref[...] = (matmul(pick_a[...], dst) * matmul(pick_b[...], src)).astype(BF16)


def holder_kernel(
    last,
    orb2,
    rows_ref,
    tails_ref,
    target_ref,
    wlr_ref,
    cg_ref,
    cg_t,
    pairs_ref,
    place_ref,
    *refs,
):
    if last:
        err_ref, before_ref, back_ref, grad_ref, dlr = refs
    else:
        back_ref, grad_ref, err_ref, dlr = refs
    step = pl.program_id(0)
    capacity = tails_ref.shape[1] - TAIL
    width = GROUP * capacity
    channels = rows_ref.shape[2]
    rows = cg_ref.shape[0]
    kinds = 3
    second = rows_ref[:, :capacity, :].reshape(width, channels)
    line = lax.broadcasted_iota(jnp.int32, (GROUP * TAIL, width), 0)
    start = place_ref[0:1, :]
    lane = lax.broadcasted_iota(jnp.int32, (LANES, width), 0)
    spread = indicator(lane == place_ref[1:2, :] + (capacity if last else 0))
    tails = tails_ref[:, capacity:, :].reshape(GROUP * TAIL, LANES)
    tags = matmul(tails, spread)
    tag_dst = jnp.sum(jnp.where(line == start, tags, 0.0), axis=0, keepdims=True)
    tag_src = jnp.sum(jnp.where(line == start + 1, tags, 0.0), axis=0, keepdims=True)
    code = jnp.where(tag_dst > 0.5, (tag_dst - 1.0) * kinds + (tag_src - 1.0), -1.0)
    code = code.astype(jnp.int32)
    pair_line = lax.broadcasted_iota(jnp.int32, (pairs_ref.shape[1], width), 0)
    pair = indicator(pair_line == code)
    both = matmul_nt(wlr_ref[...], second)
    left = both[:rows]
    right = both[rows:]
    predicted = matmul(cg_t[...], (left * right).astype(BF16))
    mask = matmul(pairs_ref[...], pair)
    resid = mask * (predicted - target_ref[...].astype(F32))
    error = jnp.sum(resid * resid, axis=0, keepdims=True) / orb2
    dpred = (resid * (1.0 / orb2)).astype(BF16)
    dcoupled = matmul(cg_ref[...], dpred)
    dlr[:rows] = (dcoupled * right).astype(BF16)
    dlr[rows:] = (dcoupled * left).astype(BF16)
    moved = matmul_tn(dlr[...], wlr_ref[...]).astype(BF16)
    for q in range(GROUP):
        back_ref[q, :capacity, :] = moved[q * capacity : (q + 1) * capacity]
    if last:

        def spell(values, spread):
            high = values.astype(BF16).astype(F32)
            middle = (values - high).astype(BF16).astype(F32)
            low = values - high - middle
            packed = jnp.where(line == start + 2, low, 0.0)
            packed = jnp.where(line == start + 1, middle, packed)
            packed = jnp.where(line == start, high, packed)
            return matmul_nt(packed.astype(BF16), spread)

        spelled = spell(err_ref[...], indicator(lane == place_ref[1:2, :]))
        spelled = (spelled + spell(error, spread)).astype(BF16)
        for q in range(GROUP):
            back_ref[q, capacity:, :] = spelled[q * TAIL : (q + 1) * TAIL]
    else:
        err_ref[...] = error
    grad = matmul(dlr[...], second)

    @pl.when(step == 0)
    def _():
        grad_ref[...] = before_ref[...] + grad if last else grad

    @pl.when(step > 0)
    def _():
        grad_ref[...] += grad


def collect_kernel(back_ref, holder_ref, rank_ref, dsecond, onehot):
    step = pl.program_id(0)
    capacity = back_ref.shape[1]
    slot_onehot(onehot, holder_ref[...], rank_ref[...], step * GROUP, capacity)
    rows = back_ref[...].reshape(GROUP * capacity, back_ref.shape[2])
    found = matmul_tn(rows, onehot[...])

    @pl.when(step == 0)
    def _():
        dsecond[...] = found

    @pl.when(step > 0)
    def _():
        dsecond[...] += found


def finish_kernel(
    back_ref,
    before_ref,
    holder_ref,
    rank_ref,
    xdst_ref,
    xsrc_ref,
    attr_ref,
    first_ref,
    pre_ref,
    mixpre_ref,
    wmix,
    grad_ref,
    error_ref,
    onehot,
    dsecond,
    found,
):
    step = pl.program_id(0)
    capacity = back_ref.shape[1] - TAIL
    edges = holder_ref.shape[1]
    channels = back_ref.shape[2]
    holder = holder_ref[...]
    rank = rank_ref[...]

    @pl.when(step == 0)
    def _():
        dsecond[...] = before_ref[...]
        found[...] = jnp.zeros_like(found)

    slot_onehot(onehot, holder, rank - capacity, step * GROUP, capacity)
    rows = back_ref[:, :capacity, :].reshape(GROUP * capacity, channels)
    dsecond[...] += matmul_tn(rows, onehot[...])
    line = lax.broadcasted_iota(jnp.int32, (GROUP * TAIL, edges), 0)
    low = (holder - step * GROUP) * TAIL
    at_holder = indicator(jnp.logical_and(line >= low, line < low + TAIL))
    tails = back_ref[:, capacity:, :].reshape(GROUP * TAIL, LANES)
    found[...] += matmul_tn(tails, at_holder)

    @pl.when(step == pl.num_programs(0) - 1)
    def _():
        place = lax.broadcasted_iota(jnp.int32, found.shape, 0)
        error_ref[...] = jnp.sum(
            jnp.where(place == rank, found[...], 0.0), axis=0, keepdims=True
        )
        dsec = dsecond[...]
        mixpre = mixpre_ref[...]
        dmix = (dsec * slope(mixpre, jax.nn.sigmoid(mixpre))).astype(BF16)
        dfirst = dsec + matmul(wmix[...], dmix)
        pre = pre_ref[...]
        dpre = (dfirst * slope(pre, jax.nn.sigmoid(pre))).astype(BF16)
        grad_ref[0:channels] = matmul_nt(xdst_ref[...], dpre)
        grad_ref[channels : 2 * channels] = matmul_nt(xsrc_ref[...], dpre)
        grad_ref[2 * channels : 3 * channels] = matmul(dpre, attr_ref[...]).T
        grad_ref[3 * channels : 4 * channels] = matmul_nt(first_ref[...], dmix)


def exchange(array, axis, groups=None):
    return lax.all_to_all(
        array, axis, split_axis=0, concat_axis=0, tiled=True, axis_index_groups=groups
    )


WIDE, NARROW, DEEP = 4, 4, 8
PEERS = WIDE * NARROW
SWAP = [(i, i ^ 1) for i in range(WIDE * 2)]
PLANE = [
    [(y * 2 + c) * NARROW * DEEP + z * NARROW + x for y in range(WIDE) for x in range(NARROW)]
    for c in range(2)
    for z in range(DEEP)
]
COLUMN = [[z * NARROW + x for z in range(DEEP)] for x in range(NARROW)]


def sum_planes(part, core):
    half = part.shape[0] // 2
    keep = lax.dynamic_slice_in_dim(part, core * half, half, 0)
    give = lax.dynamic_slice_in_dim(part, (1 - core) * half, half, 0)
    part = keep + lax.ppermute(give, "rep", SWAP)
    got = exchange(part, ("rep", "edge"), PLANE)
    return jnp.sum(got.reshape(PEERS, half // PEERS, -1), axis=0)


def sum_columns(part, core):
    got = exchange(jnp.tile(part, (DEEP, 1)), "edge", COLUMN)
    part = jnp.sum(got.reshape(DEEP, *part.shape), axis=0)
    part = exchange(jnp.tile(part, (PEERS, 1)), ("rep", "edge"), PLANE)
    other = lax.ppermute(part, "rep", SWAP)
    low = jnp.where(core == 0, part, other)
    high = jnp.where(core == 0, other, part)
    return low, high


def local(
    node_feats,
    edge_attr,
    edge_src,
    edge_dst,
    species,
    orbital_mask,
    tile_owner,
    target_send,
    w_dst,
    w_src,
    w_attr,
    w_mix,
    w_left,
    w_right,
    cg_basis,
):
    atoms, channels = node_feats.shape[1:]
    edges = edge_attr.shape[1]
    orb2, columns = target_send.shape[1:]
    devices = lax.axis_size("edge")
    capacity = columns // devices // 2
    steps = devices // GROUP
    width = GROUP * capacity
    position = lax.axis_index("edge")
    core = lax.rem(lax.axis_index("rep"), 2)
    rows = -(-orb2 // 32) * 32
    nodes = node_feats[0]
    node_lo = lax.ppermute(nodes, "edge", ring(devices, 1))
    node_hi = lax.ppermute(nodes, "edge", ring(devices, -1))
    holder = tile_owner.reshape(1, edges)
    attr = edge_attr[0]
    params = pltpu.CompilerParams(vmem_limit_bytes=VMEM)

    def whole(shape):
        return pl.BlockSpec(shape, lambda *_: (0,) * len(shape))

    def kinds_of(shift):
        return pl.BlockSpec(
            (1, atoms), lambda i, pos: (0, jnp.clip(pos[0] + shift, 0, devices - 1))
        )

    def blocks(length):
        return pl.BlockSpec((GROUP, length, channels), lambda i, *_: (i, 0, 0))

    def packets(length):
        return jax.ShapeDtypeStruct((devices, length, channels), BF16)

    def array(shape, dtype=BF16):
        return jax.ShapeDtypeStruct(shape, dtype)

    square = whole((channels, channels))
    line = whole((1, edges))
    wide = whole((channels, edges))
    onehot = pltpu.VMEM((width, edges), BF16)
    early, rank, xdst, xsrc, first, pre, mixpre, second = pl.pallas_call(
        edge_kernel,
        out_shape=(
            packets(capacity + TAIL),
            array((1, edges), jnp.int32),
            array((channels, edges)),
            array((channels, edges)),
            array((channels, edges)),
            array((channels, edges), F32),
            array((channels, edges), F32),
            array((channels, edges)),
        ),
        grid_spec=pltpu.PrefetchScalarGridSpec(
            num_scalar_prefetch=1,
            grid=(steps,),
            in_specs=[line, line, line, kinds_of(-1), kinds_of(0), kinds_of(1)]
            + [whole((atoms, channels))] * 3
            + [whole((edges, channels))]
            + [square] * 4,
            out_specs=[blocks(capacity + TAIL), line] + [wide] * 6,
            scratch_shapes=[onehot, pltpu.VMEM((2 * devices, LANES), F32)],
        ),
        compiler_params=params,
    )(
        position.astype(jnp.int32)[None],
        edge_dst,
        edge_src,
        holder,
        species,
        species,
        species,
        node_lo,
        nodes,
        node_hi,
        attr,
        w_dst,
        w_src,
        w_attr,
        w_mix,
    )
    got_early = exchange(early, "edge")
    later = pl.pallas_call(
        later_kernel,
        out_shape=packets(capacity),
        grid=(steps,),
        in_specs=[line, line, wide],
        out_specs=blocks(capacity),
        scratch_shapes=[onehot],
        compiler_params=params,
    )(holder, rank, second)

    slots = np.arange(width)
    places = np.stack([slots // capacity * TAIL, slots % capacity]).astype(np.int32)
    q, k = slots % (width // 2) // capacity, slots % capacity
    moves = (q * 2 * capacity + k + slots // (width // 2) * capacity)[None].astype(np.int32)
    species_count, orbs = orbital_mask.shape
    entry = np.arange(rows)[:, None]
    orbit = np.arange(orbs)[None, :]
    valid = entry < orb2
    pick_a = (valid & (entry // orbs == orbit)).astype(BF16)
    pick_b = (valid & (entry % orbs == orbit)).astype(BF16)
    code = np.arange(TAIL)[None, :]
    kind = np.arange(species_count)[:, None]
    known = code < species_count**2
    pick_dst = (known & (code // species_count == kind)).astype(BF16)
    pick_src = (known & (code % species_count == kind)).astype(BF16)
    halves = pl.BlockSpec((rows, width // 2), lambda i: (0, i))
    prepared = [
        array((rows, columns // 2)),
        array((rows, columns // 2)),
        array((rows, rows)),
        array((rows, rows)),
        array((2 * rows, channels)),
        array((rows, TAIL)),
    ]
    goal_early, goal_later, cg, cg_t, wlr, pairs = pl.pallas_call(
        prepare_kernel,
        out_shape=prepared,
        grid=(columns // width,),
        in_specs=[pl.BlockSpec((1, orb2, width), lambda i: (0, 0, i)), whole((1, width))]
        + [whole(a.shape) for a in (cg_basis, w_left, w_right, orbital_mask)]
        + [whole(a.shape) for a in (pick_a, pick_b, pick_dst, pick_src)],
        out_specs=[halves, halves] + [whole(a.shape) for a in prepared[2:]],
        compiler_params=params,
    )(
        target_send,
        moves,
        cg_basis,
        w_left,
        w_right,
        orbital_mask,
        pick_a,
        pick_b,
        pick_dst,
        pick_src,
    )

    later, goal_early = lax.optimization_barrier((later, goal_early))
    got_later = exchange(later, "edge")
    shared = (wlr, cg, cg_t, pairs, places)
    grad_shape = array((2 * rows, channels), F32)
    error_line = pl.BlockSpec((1, width), lambda i: (0, i))
    holder_specs = [
        pl.BlockSpec((rows, width), lambda i: (0, i)),
        *[whole(a.shape) for a in shared],
    ]
    dlr = pltpu.VMEM((2 * rows, width), BF16)
    back_early, grad_early, error_early = pl.pallas_call(
        functools.partial(holder_kernel, False, orb2),
        out_shape=(packets(capacity), grad_shape, array((1, devices * capacity), F32)),
        grid=(steps,),
        in_specs=[blocks(capacity + TAIL), blocks(capacity + TAIL), *holder_specs],
        out_specs=[blocks(capacity), whole(grad_shape.shape), error_line],
        scratch_shapes=[dlr],
        compiler_params=params,
    )(got_early, got_early, goal_early, *shared)
    returned_early = exchange(back_early, "edge")
    back_later, grad_wide = pl.pallas_call(
        functools.partial(holder_kernel, True, orb2),
        out_shape=(packets(capacity + TAIL), grad_shape),
        grid=(steps,),
        in_specs=[
            blocks(capacity),
            blocks(capacity + TAIL),
            *holder_specs,
            error_line,
            whole(grad_shape.shape),
        ],
        out_specs=[blocks(capacity + TAIL), whole(grad_shape.shape)],
        scratch_shapes=[dlr],
        compiler_params=params,
    )(got_later, got_early, goal_later, *shared, error_early, grad_early)
    returned_later = exchange(back_later, "edge")

    dsecond = pl.pallas_call(
        collect_kernel,
        out_shape=array((channels, edges), F32),
        grid=(steps,),
        in_specs=[blocks(capacity), line, line],
        out_specs=wide,
        scratch_shapes=[onehot],
        compiler_params=params,
    )(returned_early, holder, rank)
    grad_small, errors = pl.pallas_call(
        finish_kernel,
        out_shape=(array((4 * channels, channels), F32), array((1, edges), F32)),
        grid=(steps,),
        in_specs=[blocks(capacity + TAIL), wide, line, line, wide, wide]
        + [whole((edges, channels)), wide, wide, wide, square],
        out_specs=[whole((4 * channels, channels)), line],
        scratch_shapes=[
            onehot,
            pltpu.VMEM((channels, edges), F32),
            pltpu.VMEM((LANES, edges), F32),
        ],
        compiler_params=params,
    )(returned_later, dsecond, holder, rank, xdst, xsrc, attr, first, pre, mixpre, w_mix)

    unit = 2 * PEERS * 8
    full = -(-2 * rows // unit) * unit
    grad_wide = jnp.pad(grad_wide, ((0, full - 2 * rows), (0, 0)))
    part_wide = sum_planes(grad_wide, core)
    part_small = sum_planes(grad_small, core)
    split = part_wide.shape[0]
    parts = sum_columns(jnp.concatenate([part_wide, part_small], axis=0), core)
    parts = [p.reshape(PEERS, -1, channels) for p in parts]
    wide_sum = jnp.concatenate([p[:, :split].reshape(-1, channels) for p in parts], axis=0)
    small_sum = jnp.concatenate([p[:, split:].reshape(-1, channels) for p in parts], axis=0)
    outs = [small_sum[i * channels : (i + 1) * channels] for i in range(4)]
    outs += [wide_sum[i * rows :][:orb2] for i in range(2)]
    return (*outs, errors)


def solution(mesh):
    return jax.shard_map(
        local,
        mesh=mesh,
        in_specs=(
            P("rep", "edge", None),
            P("rep", "edge", None),
            P("rep", "edge"),
            P("rep", "edge"),
            P("rep", None),
            P(),
            P("rep", "edge", None),
            P("rep", "edge", None),
            P(),
            P(),
            P(),
            P(),
            P(),
            P(),
            P(),
        ),
        out_specs=(P(), P(), P(), P(), P(), P(), P("rep", "edge")),
        check_vma=False,
    )
```

```python
import functools

import jax
import jax.numpy as jnp
import numpy as np
from jax import lax
from jax.experimental import pallas as pl
from jax.experimental.pallas import tpu as pltpu
from jax.sharding import PartitionSpec as P

F32 = jnp.float32
BF16 = jnp.bfloat16
GROUP = 8
TAIL = 16
LANES = 128
CHUNK = 256
KINDS = 3
VMEM = 60 << 20


def matmul(a, b):
    return jnp.dot(a, b, preferred_element_type=F32)


def matmul_nt(a, b):
    return lax.dot_general(a, b, (((1,), (1,)), ((), ())), preferred_element_type=F32)


def matmul_tn(a, b):
    return lax.dot_general(a, b, (((0,), (0,)), ((), ())), preferred_element_type=F32)


def indicator(condition):
    return jnp.where(condition, 1.0, 0.0).astype(BF16)


def slope(value, sigma):
    return sigma * (1.0 + value * (1.0 - sigma))


def slot_onehot(out, holder, rank, base, capacity):
    edges = holder.shape[1]
    place = lax.broadcasted_iota(jnp.int32, (capacity, edges), 0)
    for p in range(GROUP):
        mine = jnp.where(holder == base + p, rank, -1)
        out[p * capacity : (p + 1) * capacity, :] = indicator(place == mine)


def table_kernel(nodes_ref, species_ref, out_ref):
    atoms, channels = nodes_ref.shape
    out_ref[:channels] = nodes_ref[...].T
    kinds = jnp.broadcast_to((species_ref[...] + 1).astype(F32), (TAIL, atoms))
    out_ref[channels:] = kinds.astype(BF16)


def edge_kernel(
    pos_ref, dst_ref, src_ref, holder_ref, attr_ref, out_ref, rank_ref, onehot, tags, *, atoms
):
    step = pl.program_id(0)
    edges = dst_ref.shape[1]
    devices = tags.shape[0] // 4
    capacity = out_ref.shape[1] - TAIL
    holder = holder_ref[...]

    @pl.when(step == 0)
    def _():
        same = lax.broadcasted_iota(jnp.int32, (devices, edges), 0) == holder
        named = jnp.where(same, 1.0, 0.0)
        named_bf = named.astype(BF16)
        rows = lax.broadcasted_iota(jnp.int32, (CHUNK, CHUNK), 0)
        cols = lax.broadcasted_iota(jnp.int32, (CHUNK, CHUNK), 1)
        earlier = indicator(rows < cols)
        carry = jnp.zeros((devices, 1), F32)
        for c in range(edges // CHUNK):
            part = slice(c * CHUNK, (c + 1) * CHUNK)
            before = matmul(named_bf[:, part], earlier) + carry
            carry = carry + jnp.sum(named[:, part], axis=1, keepdims=True)
            rank_ref[:, part] = jnp.sum(
                before * named[:, part], axis=0, keepdims=True
            ).astype(jnp.int32)
        offset = pos_ref[0] * atoms
        dst = dst_ref[...] - offset
        src = src_ref[...] - (offset - atoms)
        first = jnp.where(src >= 2 * atoms, 2, jnp.where(src >= atoms, 1, 0))
        within = src - first * atoms
        tagged = jnp.concatenate(
            [named * dst.astype(F32), named * first.astype(F32), named * within.astype(F32), named],
            axis=0,
        ).astype(BF16)
        at_rank = indicator(lax.broadcasted_iota(jnp.int32, (LANES, edges), 0) == rank_ref[...])
        tags[...] = matmul_nt(tagged, at_rank)

    slot_onehot(onehot, holder, rank_ref[...], step * GROUP, capacity)
    moved = matmul(onehot[...], attr_ref[...]).astype(BF16)
    line = lax.broadcasted_iota(jnp.int32, (TAIL, LANES), 0)
    for p in range(GROUP):
        out_ref[p, :capacity, :] = moved[p * capacity : (p + 1) * capacity]
        tail = jnp.zeros((TAIL, LANES), F32)
        for i in range(4):
            tail = jnp.where(line == i, tags[pl.ds(i * devices + step * GROUP + p, 1), :], tail)
        out_ref[p, capacity:, :] = tail.astype(BF16)


def prepare_kernel(
    cg_ref,
    wleft_ref,
    wright_ref,
    mask_ref,
    pick_a,
    pick_b,
    pick_dst,
    pick_src,
    cg_out,
    cg_t,
    wlr_out,
    wlr_t,
    pairs_ref,
):
    rows = cg_out.shape[0]
    orb2 = cg_ref.shape[0]

    def pad_rows(array):
        empty = jnp.zeros((rows - orb2, array.shape[1]), F32)
        return jnp.concatenate([array.astype(F32), empty], axis=0)

    tall = pad_rows(cg_ref[...])
    across = jnp.concatenate([tall, jnp.zeros((rows, rows - orb2), F32)], axis=1)
    cg_out[...] = across.astype(BF16)
    cg_t[...] = across.T.astype(BF16)
    both = jnp.concatenate([pad_rows(wleft_ref[...]), pad_rows(wright_ref[...])], axis=0)
    wlr_out[...] = both.astype(BF16)
    wlr_t[...] = both.T.astype(BF16)
    carried = mask_ref[...].astype(F32).astype(BF16)
    dst = matmul_tn(carried, pick_dst[...]).astype(BF16)
    src = matmul_tn(carried, pick_src[...]).astype(BF16)
    pairs_ref[...] = (matmul(pick_a[...], dst) * matmul(pick_b[...], src)).astype(BF16)


def holder_kernel(
    recv_ref,
    target_ref,
    table_ref,
    w_dst,
    w_src,
    w_attr,
    w_mix,
    wlr_ref,
    wlr_t,
    cg_ref,
    cg_t,
    pairs_ref,
    place_ref,
    grad_ref,
    err_ref,
    dlr,
):
    step = pl.program_id(0)
    steps = pl.num_programs(0)
    capacity = recv_ref.shape[1] - TAIL
    width = GROUP * capacity
    channels = recv_ref.shape[2]
    rows = cg_ref.shape[0]
    orb2 = target_ref.shape[1]
    tall = channels + TAIL
    atoms = table_ref.shape[1]

    @pl.when(step == 0)
    def _():
        grad_ref[...] = jnp.zeros_like(grad_ref)

    ids = lax.broadcasted_iota(jnp.int32, (3 * atoms, 2 * capacity), 0)
    from_dst = []
    from_src = []
    for i in range(GROUP):
        tail = recv_ref[i, capacity:, :].astype(F32)[:, :capacity]
        absent = (tail[3:4] - 1.0) * (4.0 * atoms)
        dst = tail[0:1] + (atoms + absent)
        src = tail[1:2] * atoms + tail[2:3] + absent
        place = jnp.concatenate([src, dst], axis=1).astype(jnp.int32)
        q = step * GROUP + i
        window = []
        for near in (jnp.maximum(q - 1, 0), q, jnp.minimum(q + 1, steps * GROUP - 1)):
            start = pl.multiple_of(near * tall, TAIL)
            window.append(table_ref[pl.ds(start, tall), :])
        found = matmul(jnp.concatenate(window, axis=1), indicator(ids == place))
        from_src.append(found[:, :capacity])
        from_dst.append(found[:, capacity:])
    from_dst = jnp.concatenate(from_dst, axis=1)
    from_src = jnp.concatenate(from_src, axis=1)
    xdst = from_dst[:channels].astype(BF16)
    xsrc = from_src[:channels].astype(BF16)
    kind_dst = from_dst[channels : channels + 1]
    kind_src = from_src[channels : channels + 1]
    code = jnp.where(kind_dst > 0.5, (kind_dst - 1.0) * KINDS + (kind_src - 1.0), -1.0)
    pair_line = lax.broadcasted_iota(jnp.int32, (pairs_ref.shape[1], width), 0)
    pair = indicator(pair_line == code.astype(jnp.int32))
    attr = recv_ref[:, :capacity, :].reshape(width, channels)

    pre = matmul(w_dst[...].T, xdst) + matmul(w_src[...].T, xsrc)
    pre = pre + matmul_nt(w_attr[...].T, attr)
    sig_pre = jax.nn.sigmoid(pre)
    first = (pre * sig_pre).astype(BF16)
    mixpre = matmul(w_mix[...].T, first)
    sig_mix = jax.nn.sigmoid(mixpre)
    second = (first.astype(F32) + mixpre * sig_mix).astype(BF16)

    both = matmul(wlr_ref[...], second)
    left = both[:rows]
    right = both[rows:]
    predicted = matmul(cg_t[...], (left * right).astype(BF16))
    mask = matmul(pairs_ref[...], pair)
    goal = target_ref[0].astype(F32)
    goal = jnp.concatenate([goal, jnp.zeros((rows - orb2, width), F32)], axis=0)
    resid = mask * (predicted - goal)
    error = jnp.sum(resid * resid, axis=0, keepdims=True) / orb2
    dpred = (resid * (1.0 / orb2)).astype(BF16)
    dcoupled = matmul(cg_ref[...], dpred)
    dlr[:rows] = (dcoupled * right).astype(BF16)
    dlr[rows:] = (dcoupled * left).astype(BF16)

    dsecond = matmul(wlr_t[...], dlr[...])
    dmix = (dsecond * slope(mixpre, sig_mix)).astype(BF16)
    dfirst = dsecond + matmul(w_mix[...], dmix)
    dpre = (dfirst * slope(pre, sig_pre)).astype(BF16)
    grad_ref[0:channels] += matmul_nt(xdst, dpre)
    grad_ref[channels : 2 * channels] += matmul_nt(xsrc, dpre)
    grad_ref[2 * channels : 3 * channels] += matmul(dpre, attr)
    grad_ref[3 * channels : 4 * channels] += matmul_nt(first, dmix)
    grad_ref[4 * channels : 4 * channels + 2 * rows] += matmul_nt(dlr[...], second)

    line = lax.broadcasted_iota(jnp.int32, (GROUP, width), 0)
    spread = indicator(
        lax.broadcasted_iota(jnp.int32, (LANES, width), 0) == place_ref[1:2, :]
    )
    total = jnp.zeros((GROUP, LANES), F32)
    rest = jnp.where(line == place_ref[0:1, :], error, 0.0)
    for _ in range(3):
        top = rest.astype(BF16)
        rest = rest - top.astype(F32)
        total = total + matmul_nt(top, spread)
    err_ref[...] = total

    @pl.when(step == steps - 1)
    def _():
        flipped = grad_ref[2 * channels : 3 * channels]
        grad_ref[2 * channels : 3 * channels] = flipped.T


def pick_kernel(table_ref, holder_ref, rank_ref, error_ref):
    devices, lanes = table_ref.shape
    edges = holder_ref.shape[1]
    named = indicator(
        lax.broadcasted_iota(jnp.int32, (devices, edges), 0) == holder_ref[...]
    )
    found = jnp.zeros((lanes, edges), F32)
    rest = table_ref[...]
    for _ in range(3):
        top = rest.astype(BF16)
        rest = rest - top.astype(F32)
        found = found + matmul_tn(top, named)
    place = lax.broadcasted_iota(jnp.int32, (lanes, edges), 0)
    error_ref[...] = jnp.sum(
        jnp.where(place == rank_ref[...], found, 0.0), axis=0, keepdims=True
    )


def exchange(array, axis, groups=None):
    return lax.all_to_all(
        array, axis, split_axis=0, concat_axis=0, tiled=True, axis_index_groups=groups
    )


WIDE, NARROW, DEEP = 4, 4, 8
PEERS = WIDE * NARROW
SWAP = [(i, i ^ 1) for i in range(WIDE * 2)]
PLANE = [
    [(y * 2 + c) * NARROW * DEEP + z * NARROW + x for y in range(WIDE) for x in range(NARROW)]
    for c in range(2)
    for z in range(DEEP)
]
COLUMN = [[z * NARROW + x for z in range(DEEP)] for x in range(NARROW)]
ROW = [[z * NARROW + x for x in range(NARROW)] for z in range(DEEP)]


def sum_and_return(part, errors):
    half = part.shape[0] // 2
    core = lax.rem(lax.axis_index("rep"), 2)
    row = lax.div(lax.axis_index("rep"), 2)
    length = half // PEERS
    keep = lax.dynamic_slice_in_dim(part, core * half, half, 0)
    give = lax.dynamic_slice_in_dim(part, (1 - core) * half, half, 0)
    part = keep + lax.ppermute(give, "rep", SWAP)

    lanes = errors.shape[1]
    errors = errors.reshape(DEEP, NARROW, lanes).transpose(1, 0, 2)
    errors = jnp.broadcast_to(errors[None], (WIDE, NARROW, DEEP, lanes))
    sent = jnp.concatenate(
        [part.reshape(PEERS, length, lanes), errors.reshape(PEERS, DEEP, lanes)], axis=1
    )
    got = exchange(sent, ("rep", "edge"), PLANE)
    part = jnp.sum(got[:, :length], axis=0)
    errors = lax.dynamic_slice_in_dim(got[:, length:], row * NARROW, NARROW, 0)
    errors = jnp.pad(errors.transpose(1, 0, 2), ((0, 0), (0, 8 - NARROW), (0, 0)))
    sent = jnp.concatenate(
        [jnp.broadcast_to(part[None], (DEEP, length, lanes)), errors], axis=1
    )
    got = exchange(sent, "edge", COLUMN)
    part = jnp.sum(got[:, :length], axis=0)
    errors = got[:, length : length + NARROW].reshape(DEEP * NARROW, lanes)

    part = exchange(jnp.tile(part, (PEERS, 1)), ("rep", "edge"), PLANE)
    other = lax.ppermute(part, "rep", SWAP)
    low = jnp.where(core == 0, part, other)
    high = jnp.where(core == 0, other, part)
    return jnp.concatenate([low, high], axis=0), errors


def local(
    node_feats,
    edge_attr,
    edge_src,
    edge_dst,
    species,
    orbital_mask,
    tile_owner,
    target_send,
    w_dst,
    w_src,
    w_attr,
    w_mix,
    w_left,
    w_right,
    cg_basis,
):
    atoms, channels = node_feats.shape[1:]
    edges = edge_attr.shape[1]
    orb2, columns = target_send.shape[1:]
    devices = lax.axis_size("edge")
    capacity = columns // devices
    steps = devices // GROUP
    width = GROUP * capacity
    block = capacity + TAIL
    tall = channels + TAIL
    position = lax.axis_index("edge").astype(jnp.int32)[None]
    rows = -(-orb2 // 32) * 32
    holder = tile_owner.reshape(1, edges)
    params = pltpu.CompilerParams(vmem_limit_bytes=VMEM)

    def whole(shape):
        return pl.BlockSpec(shape, lambda *_: (0,) * len(shape))

    def array(shape, dtype=BF16):
        return jax.ShapeDtypeStruct(shape, dtype)

    square = whole((channels, channels))
    line = whole((1, edges))
    packets = pl.BlockSpec((GROUP, block, channels), lambda i, *_: (i, 0, 0))

    table = pl.pallas_call(
        lambda pos_ref, *refs: table_kernel(*refs),
        out_shape=array((tall, atoms)),
        grid_spec=pltpu.PrefetchScalarGridSpec(
            num_scalar_prefetch=1,
            grid=(1,),
            in_specs=[
                whole((atoms, channels)),
                pl.BlockSpec((1, atoms), lambda i, pos: (0, pos[0])),
            ],
            out_specs=whole((tall, atoms)),
        ),
        compiler_params=params,
    )(position, node_feats[0], species)
    table = exchange(jnp.tile(table, (NARROW, 1)), "edge", ROW)
    table = lax.all_gather(table, "edge", axis=0, tiled=True, axis_index_groups=COLUMN)

    sent, rank = pl.pallas_call(
        functools.partial(edge_kernel, atoms=atoms),
        out_shape=(array((devices, block, channels)), array((1, edges), jnp.int32)),
        grid_spec=pltpu.PrefetchScalarGridSpec(
            num_scalar_prefetch=1,
            grid=(steps,),
            in_specs=[line, line, line, whole((edges, channels))],
            out_specs=[packets, line],
            scratch_shapes=[
                pltpu.VMEM((width, edges), BF16),
                pltpu.VMEM((4 * devices, LANES), F32),
            ],
        ),
        compiler_params=params,
    )(position, edge_dst, edge_src, holder, edge_attr[0])
    received = exchange(sent, "edge")

    species_count, orbs = orbital_mask.shape
    entry = np.arange(rows)[:, None]
    orbit = np.arange(orbs)[None, :]
    valid = entry < orb2
    pick_a = (valid & (entry // orbs == orbit)).astype(BF16)
    pick_b = (valid & (entry % orbs == orbit)).astype(BF16)
    code = np.arange(TAIL)[None, :]
    kind = np.arange(species_count)[:, None]
    known = code < species_count**2
    pick_dst = (known & (code // species_count == kind)).astype(BF16)
    pick_src = (known & (code % species_count == kind)).astype(BF16)
    prepared = [
        array((rows, rows)),
        array((rows, rows)),
        array((2 * rows, channels)),
        array((channels, 2 * rows)),
        array((rows, TAIL)),
    ]
    ready = pl.pallas_call(prepare_kernel, out_shape=prepared, compiler_params=params)(
        cg_basis, w_left, w_right, orbital_mask, pick_a, pick_b, pick_dst, pick_src
    )
    cg, cg_t, wlr, wlr_t, pairs = ready

    slots = np.arange(width)
    places = np.stack([slots // capacity, slots % capacity]).astype(np.int32)
    unit = 2 * PEERS * 8
    total = -(-(4 * channels + 2 * rows) // unit) * unit
    shared = (wlr, wlr_t, cg, cg_t, pairs, places)
    grads, errors = pl.pallas_call(
        holder_kernel,
        out_shape=(array((total, channels), F32), array((devices, LANES), F32)),
        grid=(steps,),
        in_specs=[
            packets,
            pl.BlockSpec((1, orb2, width), lambda i: (0, 0, i)),
            whole(table.shape),
            square,
            square,
            square,
            square,
            *[whole(a.shape) for a in shared],
        ],
        out_specs=[whole((total, channels)), pl.BlockSpec((GROUP, LANES), lambda i: (i, 0))],
        scratch_shapes=[pltpu.VMEM((2 * rows, width), BF16)],
        compiler_params=params,
    )(received, target_send, table, w_dst, w_src, w_attr, w_mix, *shared)

    grads, errors = sum_and_return(grads, errors)
    edge_error = pl.pallas_call(
        pick_kernel,
        out_shape=array((1, edges), F32),
        compiler_params=params,
    )(errors, holder, rank)
    outs = [grads[i * channels : (i + 1) * channels] for i in range(4)]
    outs += [grads[4 * channels + i * rows :][:orb2] for i in range(2)]
    return (*outs, edge_error)


def solution(mesh):
    return jax.shard_map(
        local,
        mesh=mesh,
        in_specs=(
            P("rep", "edge", None),
            P("rep", "edge", None),
            P("rep", "edge"),
            P("rep", "edge"),
            P("rep", None),
            P(),
            P("rep", "edge", None),
            P("rep", "edge", None),
            P(),
            P(),
            P(),
            P(),
            P(),
            P(),
            P(),
        ),
        out_specs=(P(), P(), P(), P(), P(), P(), P("rep", "edge")),
        check_vma=False,
    )
```

```python
import functools

import jax
import jax.numpy as jnp
import numpy as np
from jax import lax
from jax.experimental import pallas as pl
from jax.experimental.pallas import tpu as pltpu
from jax.sharding import PartitionSpec as P

F32 = jnp.float32
BF16 = jnp.bfloat16
GROUP = 8
TAIL = 16
LANES = 128
CHUNK = 256
KINDS = 3
VMEM = 60 << 20


def ring(count, shift):
    return [(i, (i + shift) % count) for i in range(count)]


def matmul(a, b):
    return jnp.dot(a, b, preferred_element_type=F32)


def matmul_nt(a, b):
    return lax.dot_general(a, b, (((1,), (1,)), ((), ())), preferred_element_type=F32)


def matmul_tn(a, b):
    return lax.dot_general(a, b, (((0,), (0,)), ((), ())), preferred_element_type=F32)


def indicator(condition):
    return jnp.where(condition, 1.0, 0.0).astype(BF16)


def slope(value, sigma):
    return sigma * (1.0 + value * (1.0 - sigma))


def slot_onehot(out, holder, rank, base, capacity):
    edges = holder.shape[1]
    place = lax.broadcasted_iota(jnp.int32, (capacity, edges), 0).astype(BF16)
    one = jnp.ones((capacity, edges), BF16)
    for p in range(GROUP):
        mine = jnp.where(holder == base + p, rank, -1).astype(BF16)
        out[p * capacity : (p + 1) * capacity, :] = jnp.where(place == mine, one, 0.0)


def edge_kernel(
    pos_ref,
    dst_ref,
    src_ref,
    holder_ref,
    spec_lo,
    spec_mid,
    spec_hi,
    node_lo,
    node_mid,
    node_hi,
    attr_ref,
    w_dst,
    w_src,
    w_attr,
    w_mix,
    out_ref,
    rank_ref,
    xdst_ref,
    xsrc_ref,
    first_ref,
    pre_ref,
    mixpre_ref,
    second_ref,
    onehot,
    tags,
):
    step = pl.program_id(0)
    edges = dst_ref.shape[1]
    devices = tags.shape[0] // 2
    capacity = out_ref.shape[1] - TAIL
    atoms = node_mid.shape[0]
    holder = holder_ref[...]

    @pl.when(step == 0)
    def _():
        offset = pos_ref[0] * atoms
        same = lax.broadcasted_iota(jnp.int32, (devices, edges), 0) == holder
        named = jnp.where(same, 1.0, 0.0)
        named_bf = named.astype(BF16)
        rows = lax.broadcasted_iota(jnp.int32, (CHUNK, CHUNK), 0)
        cols = lax.broadcasted_iota(jnp.int32, (CHUNK, CHUNK), 1)
        earlier = indicator(rows < cols)
        carry = jnp.zeros((devices, 1), F32)
        for c in range(edges // CHUNK):
            part = slice(c * CHUNK, (c + 1) * CHUNK)
            before = matmul(named_bf[:, part], earlier) + carry
            carry = carry + jnp.sum(named[:, part], axis=1, keepdims=True)
            rank_ref[:, part] = jnp.sum(
                before * named[:, part], axis=0, keepdims=True
            ).astype(jnp.int32)
        rank = rank_ref[...]

        def table_of(nodes, spec):
            kinds = jnp.broadcast_to((spec[...] + 1).astype(F32), (TAIL, atoms)).astype(BF16)
            return jnp.concatenate([nodes[...].T, kinds], axis=0)

        table_mid = table_of(node_mid, spec_mid)
        table = jnp.concatenate(
            [table_of(node_lo, spec_lo), table_mid, table_of(node_hi, spec_hi)], axis=1
        )
        channels = node_mid.shape[1]
        ids = lax.broadcasted_iota(jnp.int32, (atoms, edges), 0)
        from_dst = matmul(table_mid, indicator(ids == dst_ref[...] - offset))
        ids = lax.broadcasted_iota(jnp.int32, (3 * atoms, edges), 0)
        from_src = matmul(table, indicator(ids == src_ref[...] - (offset - atoms)))
        xdst = from_dst[:channels].astype(BF16)
        xsrc = from_src[:channels].astype(BF16)
        xdst_ref[...] = xdst
        xsrc_ref[...] = xsrc
        pre = matmul(w_dst[...].T, xdst) + matmul(w_src[...].T, xsrc)
        pre = pre + matmul_nt(w_attr[...].T, attr_ref[...])
        pre_ref[...] = pre
        first = (pre * jax.nn.sigmoid(pre)).astype(BF16)
        first_ref[...] = first
        mixpre = matmul(w_mix[...].T, first)
        mixpre_ref[...] = mixpre
        second_ref[...] = (first.astype(F32) + mixpre * jax.nn.sigmoid(mixpre)).astype(BF16)
        tagged = jnp.concatenate(
            [named * from_dst[channels : channels + 1], named * from_src[channels : channels + 1]],
            axis=0,
        ).astype(BF16)
        at_rank = indicator(lax.broadcasted_iota(jnp.int32, (LANES, edges), 0) == rank)
        tags[...] = matmul_nt(tagged, at_rank)

    slot_onehot(onehot, holder, rank_ref[...], step * GROUP, capacity)
    moved = matmul_nt(onehot[...], second_ref[...]).astype(BF16)
    line = lax.broadcasted_iota(jnp.int32, (TAIL, LANES), 0)
    for p in range(GROUP):
        out_ref[p, :capacity, :] = moved[p * capacity : (p + 1) * capacity]
        tag_dst = tags[pl.ds(step * GROUP + p, 1), :]
        tag_src = tags[pl.ds(devices + step * GROUP + p, 1), :]
        tail = jnp.where(line == 0, tag_dst, jnp.where(line == 1, tag_src, 0.0))
        out_ref[p, capacity:, :] = tail.astype(BF16)


def prepare_kernel(
    cg_ref,
    wleft_ref,
    wright_ref,
    mask_ref,
    pick_a,
    pick_b,
    pick_dst,
    pick_src,
    cg_out,
    cg_t,
    wlr_out,
    pairs_ref,
):
    rows = cg_out.shape[0]
    orb2 = cg_ref.shape[0]

    def pad_rows(array):
        empty = jnp.zeros((rows - orb2, array.shape[1]), F32)
        return jnp.concatenate([array.astype(F32), empty], axis=0)

    tall = pad_rows(cg_ref[...])
    across = jnp.concatenate([tall, jnp.zeros((rows, rows - orb2), F32)], axis=1)
    cg_out[...] = across.astype(BF16)
    cg_t[...] = across.T.astype(BF16)
    both = jnp.concatenate([pad_rows(wleft_ref[...]), pad_rows(wright_ref[...])], axis=0)
    wlr_out[...] = both.astype(BF16)
    carried = mask_ref[...].astype(F32).astype(BF16)
    dst = matmul_tn(carried, pick_dst[...]).astype(BF16)
    src = matmul_tn(carried, pick_src[...]).astype(BF16)
    pairs_ref[...] = (matmul(pick_a[...], dst) * matmul(pick_b[...], src)).astype(BF16)


def holder_kernel(
    recv_ref,
    target_ref,
    wlr_ref,
    cg_ref,
    cg_t,
    pairs_ref,
    place_ref,
    back_ref,
    grad_ref,
    dlr,
):
    step = pl.program_id(0)
    capacity = recv_ref.shape[1] - TAIL
    width = GROUP * capacity
    channels = recv_ref.shape[2]
    rows = cg_ref.shape[0]
    orb2 = target_ref.shape[1]

    @pl.when(step == 0)
    def _():
        grad_ref[...] = jnp.zeros_like(grad_ref)

    second = recv_ref[:, :capacity, :].reshape(width, channels)
    line = lax.broadcasted_iota(jnp.int32, (GROUP * TAIL, width), 0)
    start = place_ref[0:1, :]
    spread = indicator(lax.broadcasted_iota(jnp.int32, (LANES, width), 0) == place_ref[1:2, :])
    tails = recv_ref[:, capacity:, :].reshape(GROUP * TAIL, LANES)
    tags = matmul(tails, spread)
    tag_dst = jnp.sum(jnp.where(line == start, tags, 0.0), axis=0, keepdims=True)
    tag_src = jnp.sum(jnp.where(line == start + 1, tags, 0.0), axis=0, keepdims=True)
    code = jnp.where(tag_dst > 0.5, (tag_dst - 1.0) * KINDS + (tag_src - 1.0), -1.0)
    pair_line = lax.broadcasted_iota(jnp.int32, (pairs_ref.shape[1], width), 0)
    pair = indicator(pair_line == code.astype(jnp.int32))

    both = matmul_nt(wlr_ref[...], second)
    left = both[:rows]
    right = both[rows:]
    predicted = matmul(cg_t[...], (left * right).astype(BF16))
    mask = matmul(pairs_ref[...], pair)
    goal = target_ref[0].astype(F32)
    goal = jnp.concatenate([goal, jnp.zeros((rows - orb2, width), F32)], axis=0)
    resid = mask * (predicted - goal)
    error = jnp.sum(resid * resid, axis=0, keepdims=True) / orb2
    dpred = (resid * (1.0 / orb2)).astype(BF16)
    dcoupled = matmul(cg_ref[...], dpred)
    dlr[:rows] = (dcoupled * right).astype(BF16)
    dlr[rows:] = (dcoupled * left).astype(BF16)
    moved = matmul_tn(dlr[...], wlr_ref[...]).astype(BF16)
    for q in range(GROUP):
        back_ref[q, :capacity, :] = moved[q * capacity : (q + 1) * capacity]
    high = error.astype(BF16).astype(F32)
    middle = (error - high).astype(BF16).astype(F32)
    packed = jnp.where(line == start + 2, error - high - middle, 0.0)
    packed = jnp.where(line == start + 1, middle, packed)
    packed = jnp.where(line == start, high, packed).astype(BF16)
    spelled = matmul_nt(packed, spread).astype(BF16)
    for q in range(GROUP):
        back_ref[q, capacity:, :] = spelled[q * TAIL : (q + 1) * TAIL]
    grad_ref[4 * channels : 4 * channels + 2 * rows] += matmul(dlr[...], second)


def finish_kernel(
    back_ref,
    holder_ref,
    rank_ref,
    xdst_ref,
    xsrc_ref,
    attr_ref,
    first_ref,
    pre_ref,
    mixpre_ref,
    wmix,
    before_ref,
    grad_ref,
    error_ref,
    onehot,
    dsecond,
    found,
):
    step = pl.program_id(0)
    capacity = back_ref.shape[1] - TAIL
    edges = holder_ref.shape[1]
    channels = back_ref.shape[2]
    holder = holder_ref[...]
    rank = rank_ref[...]

    @pl.when(step == 0)
    def _():
        dsecond[...] = jnp.zeros_like(dsecond)
        found[...] = jnp.zeros_like(found)

    slot_onehot(onehot, holder, rank, step * GROUP, capacity)
    rows = back_ref[:, :capacity, :].reshape(GROUP * capacity, channels)
    dsecond[...] += matmul_tn(rows, onehot[...])
    line = lax.broadcasted_iota(jnp.int32, (GROUP * TAIL, edges), 0)
    low = (holder - step * GROUP) * TAIL
    at_holder = indicator(jnp.logical_and(line >= low, line < low + TAIL))
    tails = back_ref[:, capacity:, :].reshape(GROUP * TAIL, LANES)
    found[...] += matmul_tn(tails, at_holder)

    @pl.when(step == pl.num_programs(0) - 1)
    def _():
        place = lax.broadcasted_iota(jnp.int32, found.shape, 0)
        error_ref[...] = jnp.sum(
            jnp.where(place == rank, found[...], 0.0), axis=0, keepdims=True
        )
        dsec = dsecond[...]
        mixpre = mixpre_ref[...]
        dmix = (dsec * slope(mixpre, jax.nn.sigmoid(mixpre))).astype(BF16)
        dfirst = dsec + matmul(wmix[...], dmix)
        pre = pre_ref[...]
        dpre = (dfirst * slope(pre, jax.nn.sigmoid(pre))).astype(BF16)
        grad_ref[0:channels] = matmul_nt(xdst_ref[...], dpre)
        grad_ref[channels : 2 * channels] = matmul_nt(xsrc_ref[...], dpre)
        grad_ref[2 * channels : 3 * channels] = matmul(dpre, attr_ref[...]).T
        grad_ref[3 * channels : 4 * channels] = matmul_nt(first_ref[...], dmix)


def exchange(array, axis, groups=None):
    return lax.all_to_all(
        array, axis, split_axis=0, concat_axis=0, tiled=True, axis_index_groups=groups
    )


WIDE, NARROW, DEEP = 4, 4, 8
PEERS = WIDE * NARROW
SWAP = [(i, i ^ 1) for i in range(WIDE * 2)]
PLANE = [
    [(y * 2 + c) * NARROW * DEEP + z * NARROW + x for y in range(WIDE) for x in range(NARROW)]
    for c in range(2)
    for z in range(DEEP)
]
COLUMN = [[z * NARROW + x for z in range(DEEP)] for x in range(NARROW)]


def sum_everywhere(part):
    half = part.shape[0] // 2
    core = lax.rem(lax.axis_index("rep"), 2)
    keep = lax.dynamic_slice_in_dim(part, core * half, half, 0)
    give = lax.dynamic_slice_in_dim(part, (1 - core) * half, half, 0)
    part = keep + lax.ppermute(give, "rep", SWAP)
    got = exchange(part, ("rep", "edge"), PLANE)
    part = jnp.sum(got.reshape(PEERS, half // PEERS, -1), axis=0)
    got = exchange(jnp.tile(part, (DEEP, 1)), "edge", COLUMN)
    part = jnp.sum(got.reshape(DEEP, *part.shape), axis=0)
    part = exchange(jnp.tile(part, (PEERS, 1)), ("rep", "edge"), PLANE)
    other = lax.ppermute(part, "rep", SWAP)
    low = jnp.where(core == 0, part, other)
    high = jnp.where(core == 0, other, part)
    return jnp.concatenate([low, high], axis=0)


def local(
    node_feats,
    edge_attr,
    edge_src,
    edge_dst,
    species,
    orbital_mask,
    tile_owner,
    target_send,
    w_dst,
    w_src,
    w_attr,
    w_mix,
    w_left,
    w_right,
    cg_basis,
):
    atoms, channels = node_feats.shape[1:]
    edges = edge_attr.shape[1]
    orb2, columns = target_send.shape[1:]
    devices = lax.axis_size("edge")
    capacity = columns // devices
    steps = devices // GROUP
    width = GROUP * capacity
    block = capacity + TAIL
    position = lax.axis_index("edge").astype(jnp.int32)[None]
    nodes = node_feats[0]
    node_lo = lax.ppermute(nodes, "edge", ring(devices, 1))
    node_hi = lax.ppermute(nodes, "edge", ring(devices, -1))
    attr = edge_attr[0]
    rows = -(-orb2 // 32) * 32
    holder = tile_owner.reshape(1, edges)
    params = pltpu.CompilerParams(vmem_limit_bytes=VMEM)

    def whole(shape):
        return pl.BlockSpec(shape, lambda *_: (0,) * len(shape))

    def array(shape, dtype=BF16):
        return jax.ShapeDtypeStruct(shape, dtype)

    square = whole((channels, channels))
    line = whole((1, edges))
    packets = pl.BlockSpec((GROUP, block, channels), lambda i, *_: (i, 0, 0))

    wide = whole((channels, edges))
    onehot = pltpu.VMEM((width, edges), BF16)

    def kinds_of(shift):
        return pl.BlockSpec(
            (1, atoms), lambda i, pos: (0, jnp.clip(pos[0] + shift, 0, devices - 1))
        )

    sent, rank, xdst, xsrc, first, pre, mixpre = pl.pallas_call(
        edge_kernel,
        out_shape=(
            array((devices, block, channels)),
            array((1, edges), jnp.int32),
            array((channels, edges)),
            array((channels, edges)),
            array((channels, edges)),
            array((channels, edges), F32),
            array((channels, edges), F32),
        ),
        grid_spec=pltpu.PrefetchScalarGridSpec(
            num_scalar_prefetch=1,
            grid=(steps,),
            in_specs=[line, line, line, kinds_of(-1), kinds_of(0), kinds_of(1)]
            + [whole((atoms, channels))] * 3
            + [whole((edges, channels))]
            + [square] * 4,
            out_specs=[packets, line] + [wide] * 5,
            scratch_shapes=[
                pltpu.VMEM((channels, edges), BF16),
                onehot,
                pltpu.VMEM((2 * devices, LANES), F32),
            ],
        ),
        compiler_params=params,
    )(
        position,
        edge_dst,
        edge_src,
        holder,
        species,
        species,
        species,
        node_lo,
        nodes,
        node_hi,
        attr,
        w_dst,
        w_src,
        w_attr,
        w_mix,
    )
    received = exchange(sent, "edge")

    species_count, orbs = orbital_mask.shape
    entry = np.arange(rows)[:, None]
    orbit = np.arange(orbs)[None, :]
    valid = entry < orb2
    pick_a = (valid & (entry // orbs == orbit)).astype(BF16)
    pick_b = (valid & (entry % orbs == orbit)).astype(BF16)
    code = np.arange(TAIL)[None, :]
    kind = np.arange(species_count)[:, None]
    known = code < species_count**2
    pick_dst = (known & (code // species_count == kind)).astype(BF16)
    pick_src = (known & (code % species_count == kind)).astype(BF16)
    prepared = [
        array((rows, rows)),
        array((rows, rows)),
        array((2 * rows, channels)),
        array((rows, TAIL)),
    ]
    ready = pl.pallas_call(prepare_kernel, out_shape=prepared, compiler_params=params)(
        cg_basis, w_left, w_right, orbital_mask, pick_a, pick_b, pick_dst, pick_src
    )
    cg, cg_t, wlr, pairs = ready

    slots = np.arange(width)
    places = np.stack([slots // capacity * TAIL, slots % capacity]).astype(np.int32)
    unit = 2 * PEERS * 8
    total = -(-(4 * channels + 2 * rows) // unit) * unit
    shared = (wlr, cg, cg_t, pairs, places)
    back, grads = pl.pallas_call(
        holder_kernel,
        out_shape=(array((devices, block, channels)), array((total, channels), F32)),
        grid=(steps,),
        in_specs=[
            packets,
            pl.BlockSpec((1, orb2, width), lambda i: (0, 0, i)),
            *[whole(a.shape) for a in shared],
        ],
        out_specs=[packets, whole((total, channels))],
        scratch_shapes=[pltpu.VMEM((2 * rows, width), BF16)],
        compiler_params=params,
    )(received, target_send, *shared)
    returned = exchange(back, "edge")

    grads, errors = pl.pallas_call(
        finish_kernel,
        out_shape=(array((total, channels), F32), array((1, edges), F32)),
        grid=(steps,),
        in_specs=[packets, line, line, wide, wide, whole((edges, channels))]
        + [wide, wide, wide, square, pl.BlockSpec(memory_space=pl.ANY)],
        out_specs=[whole((4 * channels, channels)), line],
        scratch_shapes=[
            onehot,
            pltpu.VMEM((channels, edges), F32),
            pltpu.VMEM((LANES, edges), F32),
        ],
        input_output_aliases={10: 0},
        compiler_params=params,
    )(returned, holder, rank, xdst, xsrc, attr, first, pre, mixpre, w_mix, grads)

    grads = sum_everywhere(grads)
    outs = [grads[i * channels : (i + 1) * channels] for i in range(4)]
    outs += [grads[4 * channels + i * rows :][:orb2] for i in range(2)]
    return (*outs, errors)


def solution(mesh):
    return jax.shard_map(
        local,
        mesh=mesh,
        in_specs=(
            P("rep", "edge", None),
            P("rep", "edge", None),
            P("rep", "edge"),
            P("rep", "edge"),
            P("rep", None),
            P(),
            P("rep", "edge", None),
            P("rep", "edge", None),
            P(),
            P(),
            P(),
            P(),
            P(),
            P(),
            P(),
        ),
        out_specs=(P(), P(), P(), P(), P(), P(), P("rep", "edge")),
        check_vma=False,
    )
```

```python
import functools

import jax
import jax.numpy as jnp
import numpy as np
from jax import lax
from jax.experimental import pallas as pl
from jax.experimental.pallas import tpu as pltpu
from jax.sharding import PartitionSpec as P

F32 = jnp.float32
BF16 = jnp.bfloat16
GROUP = 8
EDGE_GROUP = 16
TAIL = 16
LANES = 128
CHUNK = 256
KINDS = 3
VMEM = 60 << 20


def ring(count, shift):
    return [(i, (i + shift) % count) for i in range(count)]


def matmul(a, b):
    return jnp.dot(a, b, preferred_element_type=F32)


def matmul_nt(a, b):
    return lax.dot_general(a, b, (((1,), (1,)), ((), ())), preferred_element_type=F32)


def matmul_tn(a, b):
    return lax.dot_general(a, b, (((0,), (0,)), ((), ())), preferred_element_type=F32)


def indicator(condition):
    return jnp.where(condition, 1.0, 0.0).astype(BF16)


def slope(value, sigma):
    return sigma * (1.0 + value * (1.0 - sigma))


def layers(xdst, xsrc, attr_ref, w_dst, w_src, w_attr, w_mix):
    pre = matmul(w_dst[...].T, xdst) + matmul(w_src[...].T, xsrc)
    pre = pre + matmul_nt(w_attr[...].T, attr_ref[...])
    first = (pre * jax.nn.sigmoid(pre)).astype(BF16)
    return pre, first, matmul(w_mix[...].T, first)


def slot_onehot(out, holder, rank, base, capacity):
    edges = holder.shape[1]
    place = lax.broadcasted_iota(jnp.int32, (capacity, edges), 0).astype(BF16)
    one = jnp.ones((capacity, edges), BF16)
    for p in range(EDGE_GROUP):
        mine = jnp.where(holder == base + p, rank, -1).astype(BF16)
        out[p * capacity : (p + 1) * capacity, :] = jnp.where(place == mine, one, 0.0)


def edge_kernel(
    pos_ref,
    dst_ref,
    src_ref,
    holder_ref,
    spec_lo,
    spec_mid,
    spec_hi,
    node_lo,
    node_mid,
    node_hi,
    attr_ref,
    w_dst,
    w_src,
    w_attr,
    w_mix,
    out_ref,
    rank_ref,
    xdst_ref,
    xsrc_ref,
    second_ref,
    onehot,
    tags,
):
    step = pl.program_id(0)
    edges = dst_ref.shape[1]
    devices = tags.shape[0] // 2
    capacity = out_ref.shape[1] - TAIL
    atoms = node_mid.shape[0]
    holder = holder_ref[...]

    @pl.when(step == 0)
    def _():
        offset = pos_ref[0] * atoms
        same = lax.broadcasted_iota(jnp.int32, (devices, edges), 0) == holder
        named = jnp.where(same, 1.0, 0.0)
        named_bf = named.astype(BF16)
        rows = lax.broadcasted_iota(jnp.int32, (CHUNK, CHUNK), 0)
        cols = lax.broadcasted_iota(jnp.int32, (CHUNK, CHUNK), 1)
        earlier = indicator(rows < cols)
        carry = jnp.zeros((devices, 1), F32)
        for c in range(edges // CHUNK):
            part = slice(c * CHUNK, (c + 1) * CHUNK)
            before = matmul(named_bf[:, part], earlier) + carry
            carry = carry + jnp.sum(named[:, part], axis=1, keepdims=True)
            rank_ref[:, part] = jnp.sum(
                before * named[:, part], axis=0, keepdims=True
            ).astype(jnp.int32)
        rank = rank_ref[...]

        def table_of(nodes, spec):
            kinds = jnp.broadcast_to((spec[...] + 1).astype(F32), (TAIL, atoms)).astype(BF16)
            return jnp.concatenate([nodes[...].T, kinds], axis=0)

        table_mid = table_of(node_mid, spec_mid)
        table = jnp.concatenate(
            [table_of(node_lo, spec_lo), table_mid, table_of(node_hi, spec_hi)], axis=1
        )
        channels = node_mid.shape[1]
        ids = lax.broadcasted_iota(jnp.int32, (atoms, edges), 0)
        from_dst = matmul(table_mid, indicator(ids == dst_ref[...] - offset))
        ids = lax.broadcasted_iota(jnp.int32, (3 * atoms, edges), 0)
        from_src = matmul(table, indicator(ids == src_ref[...] - (offset - atoms)))
        xdst = from_dst[:channels].astype(BF16)
        xsrc = from_src[:channels].astype(BF16)
        xdst_ref[...] = xdst
        xsrc_ref[...] = xsrc
        _, first, mixpre = layers(xdst, xsrc, attr_ref, w_dst, w_src, w_attr, w_mix)
        second_ref[...] = (first.astype(F32) + mixpre * jax.nn.sigmoid(mixpre)).astype(BF16)
        tagged = jnp.concatenate(
            [named * from_dst[channels : channels + 1], named * from_src[channels : channels + 1]],
            axis=0,
        ).astype(BF16)
        at_rank = indicator(lax.broadcasted_iota(jnp.int32, (LANES, edges), 0) == rank)
        tags[...] = matmul_nt(tagged, at_rank)

    slot_onehot(onehot, holder, rank_ref[...], step * EDGE_GROUP, capacity)
    moved = matmul_nt(onehot[...], second_ref[...]).astype(BF16)
    line = lax.broadcasted_iota(jnp.int32, (TAIL, LANES), 0)
    for p in range(EDGE_GROUP):
        out_ref[p, :capacity, :] = moved[p * capacity : (p + 1) * capacity]
        tag_dst = tags[pl.ds(step * EDGE_GROUP + p, 1), :]
        tag_src = tags[pl.ds(devices + step * EDGE_GROUP + p, 1), :]
        tail = jnp.where(line == 0, tag_dst, jnp.where(line == 1, tag_src, 0.0))
        out_ref[p, capacity:, :] = tail.astype(BF16)


def prepare_kernel(
    cg_ref,
    wleft_ref,
    wright_ref,
    mask_ref,
    pick_a,
    pick_b,
    pick_dst,
    pick_src,
    cg_out,
    cg_t,
    wlr_out,
    wlr_t,
    pairs_ref,
):
    rows = cg_out.shape[0]
    orb2 = cg_ref.shape[0]

    def pad_rows(array):
        empty = jnp.zeros((rows - orb2, array.shape[1]), F32)
        return jnp.concatenate([array.astype(F32), empty], axis=0)

    tall = pad_rows(cg_ref[...])
    across = jnp.concatenate([tall, jnp.zeros((rows, rows - orb2), F32)], axis=1)
    cg_out[...] = across.astype(BF16)
    cg_t[...] = across.T.astype(BF16)
    both = jnp.concatenate([pad_rows(wleft_ref[...]), pad_rows(wright_ref[...])], axis=0)
    wlr_out[...] = both.astype(BF16)
    wlr_t[...] = both.T.astype(BF16)
    carried = mask_ref[...].astype(F32).astype(BF16)
    dst = matmul_tn(carried, pick_dst[...]).astype(BF16)
    src = matmul_tn(carried, pick_src[...]).astype(BF16)
    pairs_ref[...] = (matmul(pick_a[...], dst) * matmul(pick_b[...], src)).astype(BF16)


def holder_kernel(
    recv_ref,
    target_ref,
    wlr_ref,
    wlr_t,
    cg_ref,
    cg_t,
    pairs_ref,
    place_ref,
    back_ref,
    grad_ref,
    dlr,
):
    step = pl.program_id(0)
    capacity = recv_ref.shape[1] - TAIL
    width = GROUP * capacity
    channels = recv_ref.shape[2]
    rows = cg_ref.shape[0]
    orb2 = target_ref.shape[1]

    @pl.when(step == 0)
    def _():
        grad_ref[...] = jnp.zeros_like(grad_ref)

    second = recv_ref[:, :capacity, :].reshape(width, channels)
    line = lax.broadcasted_iota(jnp.int32, (GROUP * TAIL, width), 0)
    start = place_ref[0:1, :]
    spread = indicator(lax.broadcasted_iota(jnp.int32, (LANES, width), 0) == place_ref[1:2, :])
    tails = recv_ref[:, capacity:, :].reshape(GROUP * TAIL, LANES)
    tags = matmul(tails, spread)
    tag_dst = jnp.sum(jnp.where(line == start, tags, 0.0), axis=0, keepdims=True)
    tag_src = jnp.sum(jnp.where(line == start + 1, tags, 0.0), axis=0, keepdims=True)
    code = jnp.where(tag_dst > 0.5, (tag_dst - 1.0) * KINDS + (tag_src - 1.0), -1.0)
    pair_line = lax.broadcasted_iota(jnp.int32, (pairs_ref.shape[1], width), 0)
    pair = indicator(pair_line == code.astype(jnp.int32))

    both = matmul_nt(wlr_ref[...], second)
    left = both[:rows]
    right = both[rows:]
    predicted = matmul(cg_t[...], (left * right).astype(BF16))
    mask = matmul(pairs_ref[...], pair)
    goal = target_ref[0].astype(F32)
    goal = jnp.concatenate([goal, jnp.zeros((rows - orb2, width), F32)], axis=0)
    resid = mask * (predicted - goal)
    error = jnp.sum(resid * resid, axis=0, keepdims=True) / orb2
    dpred = (resid * (1.0 / orb2)).astype(BF16)
    dcoupled = matmul(cg_ref[...], dpred)
    dlr[:rows] = (dcoupled * right).astype(BF16)
    dlr[rows:] = (dcoupled * left).astype(BF16)
    grad_ref[4 * channels : 4 * channels + 2 * rows] += matmul(dlr[...], second)
    moved = matmul(wlr_t[...], dlr[...]).T.astype(BF16)
    for q in range(GROUP):
        back_ref[q, :capacity, :] = moved[q * capacity : (q + 1) * capacity]
    high = error.astype(BF16).astype(F32)
    middle = (error - high).astype(BF16).astype(F32)
    packed = jnp.where(line == start + 2, error - high - middle, 0.0)
    packed = jnp.where(line == start + 1, middle, packed)
    packed = jnp.where(line == start, high, packed).astype(BF16)
    spelled = matmul_nt(packed, spread).astype(BF16)
    for q in range(GROUP):
        back_ref[q, capacity:, :] = spelled[q * TAIL : (q + 1) * TAIL]


def finish_kernel(
    back_ref,
    holder_ref,
    rank_ref,
    xdst_hbm,
    xsrc_hbm,
    attr_hbm,
    w_dst,
    w_src,
    w_attr,
    w_mix,
    before_ref,
    grad_ref,
    error_ref,
    onehot,
    dsecond,
    found,
    xdst_ref,
    xsrc_ref,
    attr_ref,
    sems,
):
    step = pl.program_id(0)
    capacity = back_ref.shape[1] - TAIL
    edges = holder_ref.shape[1]
    channels = back_ref.shape[2]
    holder = holder_ref[...]
    rank = rank_ref[...]

    wanted = ((xdst_hbm, xdst_ref), (xsrc_hbm, xsrc_ref), (attr_hbm, attr_ref))
    loads = [
        pltpu.make_async_copy(source, kept, sems.at[i])
        for i, (source, kept) in enumerate(wanted)
    ]

    @pl.when(step == 0)
    def _():
        for load in loads:
            load.start()
        dsecond[...] = jnp.zeros_like(dsecond)
        found[...] = jnp.zeros_like(found)

    slot_onehot(onehot, holder, rank, step * EDGE_GROUP, capacity)
    rows = back_ref[:, :capacity, :].reshape(EDGE_GROUP * capacity, channels)
    dsecond[...] += matmul_tn(rows, onehot[...])
    line = lax.broadcasted_iota(jnp.int32, (EDGE_GROUP * TAIL, edges), 0)
    low = (holder - step * EDGE_GROUP) * TAIL
    at_holder = indicator(jnp.logical_and(line >= low, line < low + TAIL))
    tails = back_ref[:, capacity:, :].reshape(EDGE_GROUP * TAIL, LANES)
    found[...] += matmul_tn(tails, at_holder)

    @pl.when(step == pl.num_programs(0) - 1)
    def _():
        for load in loads:
            load.wait()
        place = lax.broadcasted_iota(jnp.int32, found.shape, 0)
        error_ref[...] = jnp.sum(
            jnp.where(place == rank, found[...], 0.0), axis=0, keepdims=True
        )
        dsec = dsecond[...]
        pre, first, mixpre = layers(
            xdst_ref[...], xsrc_ref[...], attr_ref, w_dst, w_src, w_attr, w_mix
        )
        dmix = (dsec * slope(mixpre, jax.nn.sigmoid(mixpre))).astype(BF16)
        dfirst = dsec + matmul(w_mix[...], dmix)
        dpre = (dfirst * slope(pre, jax.nn.sigmoid(pre))).astype(BF16)
        grad_ref[0:channels] = matmul_nt(xdst_ref[...], dpre)
        grad_ref[channels : 2 * channels] = matmul_nt(xsrc_ref[...], dpre)
        grad_ref[2 * channels : 3 * channels] = matmul(dpre, attr_ref[...]).T
        grad_ref[3 * channels : 4 * channels] = matmul_nt(first, dmix)


def exchange(array, axis, groups=None):
    return lax.all_to_all(
        array, axis, split_axis=0, concat_axis=0, tiled=True, axis_index_groups=groups
    )


WIDE, NARROW, DEEP = 4, 4, 8
PEERS = WIDE * NARROW
SWAP = [(i, i ^ 1) for i in range(WIDE * 2)]
PLANE = [
    [(y * 2 + c) * NARROW * DEEP + z * NARROW + x for y in range(WIDE) for x in range(NARROW)]
    for c in range(2)
    for z in range(DEEP)
]
COLUMN = [[z * NARROW + x for z in range(DEEP)] for x in range(NARROW)]


def sum_everywhere(part):
    half = part.shape[0] // 2
    core = lax.rem(lax.axis_index("rep"), 2)
    keep = lax.dynamic_slice_in_dim(part, core * half, half, 0)
    give = lax.dynamic_slice_in_dim(part, (1 - core) * half, half, 0)
    part = keep + lax.ppermute(give, "rep", SWAP)
    got = exchange(part, ("rep", "edge"), PLANE)
    part = jnp.sum(got.reshape(PEERS, half // PEERS, -1), axis=0)
    got = exchange(jnp.tile(part, (DEEP, 1)), "edge", COLUMN)
    part = jnp.sum(got.reshape(DEEP, *part.shape), axis=0)
    part = exchange(jnp.tile(part, (PEERS, 1)), ("rep", "edge"), PLANE)
    other = lax.ppermute(part, "rep", SWAP)
    low = jnp.where(core == 0, part, other)
    high = jnp.where(core == 0, other, part)
    return jnp.concatenate([low, high], axis=0)


def local(
    node_feats,
    edge_attr,
    edge_src,
    edge_dst,
    species,
    orbital_mask,
    tile_owner,
    target_send,
    w_dst,
    w_src,
    w_attr,
    w_mix,
    w_left,
    w_right,
    cg_basis,
):
    atoms, channels = node_feats.shape[1:]
    edges = edge_attr.shape[1]
    orb2, columns = target_send.shape[1:]
    devices = lax.axis_size("edge")
    capacity = columns // devices
    steps = devices // GROUP
    width = GROUP * capacity
    block = capacity + TAIL
    position = lax.axis_index("edge").astype(jnp.int32)[None]
    nodes = node_feats[0]
    node_lo = lax.ppermute(nodes, "edge", ring(devices, 1))
    node_hi = lax.ppermute(nodes, "edge", ring(devices, -1))
    attr = edge_attr[0]
    rows = -(-orb2 // 32) * 32
    holder = tile_owner.reshape(1, edges)
    params = pltpu.CompilerParams(vmem_limit_bytes=VMEM)

    def whole(shape):
        return pl.BlockSpec(shape, lambda *_: (0,) * len(shape))

    def array(shape, dtype=BF16):
        return jax.ShapeDtypeStruct(shape, dtype)

    square = whole((channels, channels))
    line = whole((1, edges))
    packets = pl.BlockSpec((GROUP, block, channels), lambda i, *_: (i, 0, 0))
    edge_packets = pl.BlockSpec((EDGE_GROUP, block, channels), lambda i, *_: (i, 0, 0))

    wide = whole((channels, edges))
    edge_steps = devices // EDGE_GROUP
    onehot = pltpu.VMEM((EDGE_GROUP * capacity, edges), BF16)

    def kinds_of(shift):
        return pl.BlockSpec(
            (1, atoms), lambda i, pos: (0, jnp.clip(pos[0] + shift, 0, devices - 1))
        )

    sent, rank, xdst, xsrc = pl.pallas_call(
        edge_kernel,
        out_shape=(
            array((devices, block, channels)),
            array((1, edges), jnp.int32),
            array((channels, edges)),
            array((channels, edges)),
        ),
        grid_spec=pltpu.PrefetchScalarGridSpec(
            num_scalar_prefetch=1,
            grid=(edge_steps,),
            in_specs=[line, line, line, kinds_of(-1), kinds_of(0), kinds_of(1)]
            + [whole((atoms, channels))] * 3
            + [whole((edges, channels))]
            + [square] * 4,
            out_specs=[edge_packets, line] + [wide] * 2,
            scratch_shapes=[
                pltpu.VMEM((channels, edges), BF16),
                onehot,
                pltpu.VMEM((2 * devices, LANES), F32),
            ],
        ),
        compiler_params=params,
    )(
        position,
        edge_dst,
        edge_src,
        holder,
        species,
        species,
        species,
        node_lo,
        nodes,
        node_hi,
        attr,
        w_dst,
        w_src,
        w_attr,
        w_mix,
    )
    received = exchange(sent, "edge")

    species_count, orbs = orbital_mask.shape
    entry = np.arange(rows)[:, None]
    orbit = np.arange(orbs)[None, :]
    valid = entry < orb2
    pick_a = (valid & (entry // orbs == orbit)).astype(BF16)
    pick_b = (valid & (entry % orbs == orbit)).astype(BF16)
    code = np.arange(TAIL)[None, :]
    kind = np.arange(species_count)[:, None]
    known = code < species_count**2
    pick_dst = (known & (code // species_count == kind)).astype(BF16)
    pick_src = (known & (code % species_count == kind)).astype(BF16)
    prepared = [
        array((rows, rows)),
        array((rows, rows)),
        array((2 * rows, channels)),
        array((channels, 2 * rows)),
        array((rows, TAIL)),
    ]
    ready = pl.pallas_call(prepare_kernel, out_shape=prepared, compiler_params=pltpu.CompilerParams(vmem_limit_bytes=24 << 20))(
        cg_basis, w_left, w_right, orbital_mask, pick_a, pick_b, pick_dst, pick_src
    )
    cg, cg_t, wlr, wlr_t, pairs = ready

    slots = np.arange(width)
    places = np.stack([slots // capacity * TAIL, slots % capacity]).astype(np.int32)
    unit = 2 * PEERS * 8
    total = -(-(4 * channels + 2 * rows) // unit) * unit
    shared = (wlr, wlr_t, cg, cg_t, pairs, places)
    back, grads = pl.pallas_call(
        holder_kernel,
        out_shape=(array((devices, block, channels)), array((total, channels), F32)),
        grid=(steps,),
        in_specs=[
            packets,
            pl.BlockSpec((1, orb2, width), lambda i: (0, 0, i)),
            *[whole(a.shape) for a in shared],
        ],
        out_specs=[packets, whole((total, channels))],
        scratch_shapes=[pltpu.VMEM((2 * rows, width), BF16)],
        compiler_params=pltpu.CompilerParams(vmem_limit_bytes=52 << 20),
    )(received, target_send, *shared)
    returned = exchange(back, "edge")

    grads, errors = pl.pallas_call(
        finish_kernel,
        out_shape=(array((total, channels), F32), array((1, edges), F32)),
        grid=(edge_steps,),
        in_specs=[edge_packets, line, line]
        + [pl.BlockSpec(memory_space=pl.ANY)] * 3
        + [square] * 4
        + [pl.BlockSpec(memory_space=pl.ANY)],
        out_specs=[whole((4 * channels, channels)), line],
        scratch_shapes=[
            onehot,
            pltpu.VMEM((channels, edges), F32),
            pltpu.VMEM((LANES, edges), F32),
            pltpu.VMEM((channels, edges), BF16),
            pltpu.VMEM((channels, edges), BF16),
            pltpu.VMEM((edges, channels), BF16),
            pltpu.SemaphoreType.DMA((3,)),
        ],
        input_output_aliases={10: 0},
        compiler_params=params,
    )(returned, holder, rank, xdst, xsrc, attr, w_dst, w_src, w_attr, w_mix, grads)

    grads = sum_everywhere(grads)
    outs = [grads[i * channels : (i + 1) * channels] for i in range(4)]
    outs += [grads[4 * channels + i * rows :][:orb2] for i in range(2)]
    return (*outs, errors)


def solution(mesh):
    return jax.shard_map(
        local,
        mesh=mesh,
        in_specs=(
            P("rep", "edge", None),
            P("rep", "edge", None),
            P("rep", "edge"),
            P("rep", "edge"),
            P("rep", None),
            P(),
            P("rep", "edge", None),
            P("rep", "edge", None),
            P(),
            P(),
            P(),
            P(),
            P(),
            P(),
            P(),
        ),
        out_specs=(P(), P(), P(), P(), P(), P(), P("rep", "edge")),
        check_vma=False,
    )
```

```python
import functools

import jax
import jax.numpy as jnp
import numpy as np
from jax import lax
from jax.experimental import pallas as pl
from jax.experimental.pallas import tpu as pltpu
from jax.sharding import PartitionSpec as P

F32 = jnp.float32
BF16 = jnp.bfloat16
GROUP = 8
EDGE_GROUP = 32
TAIL = 16
LANES = 128
CHUNK = 256
KINDS = 3
VMEM = 60 << 20


def ring(count, shift):
    return [(i, (i + shift) % count) for i in range(count)]


def matmul(a, b):
    return jnp.dot(a, b, preferred_element_type=F32)


def matmul_nt(a, b):
    return lax.dot_general(a, b, (((1,), (1,)), ((), ())), preferred_element_type=F32)


def matmul_tn(a, b):
    return lax.dot_general(a, b, (((0,), (0,)), ((), ())), preferred_element_type=F32)


def indicator(condition):
    return jnp.where(condition, 1.0, 0.0).astype(BF16)


def slope(value, sigma):
    return sigma * (1.0 + value * (1.0 - sigma))


def layers(xdst, xsrc, attr_ref, w_dst, w_src, w_attr, w_mix):
    pre = matmul(w_dst[...].T, xdst) + matmul(w_src[...].T, xsrc)
    pre = pre + matmul_nt(w_attr[...].T, attr_ref[...])
    first = (pre * jax.nn.sigmoid(pre)).astype(BF16)
    return pre, first, matmul(w_mix[...].T, first)


def slot_onehot(out, holder, rank, base, capacity):
    edges = holder.shape[1]
    place = lax.broadcasted_iota(jnp.int32, (capacity, edges), 0).astype(BF16)
    one = jnp.ones((capacity, edges), BF16)
    for p in range(EDGE_GROUP):
        mine = jnp.where(holder == base + p, rank, -1).astype(BF16)
        out[p * capacity : (p + 1) * capacity, :] = jnp.where(place == mine, one, 0.0)


def edge_kernel(
    pos_ref,
    dst_ref,
    src_ref,
    holder_ref,
    spec_lo,
    spec_mid,
    spec_hi,
    node_lo,
    node_mid,
    node_hi,
    attr_ref,
    w_dst,
    w_src,
    w_attr,
    w_mix,
    out_ref,
    rank_ref,
    xdst_ref,
    xsrc_ref,
    second_ref,
    onehot,
    tags,
):
    step = pl.program_id(0)
    edges = dst_ref.shape[1]
    devices = tags.shape[0] // 2
    capacity = out_ref.shape[1] - TAIL
    atoms = node_mid.shape[0]
    holder = holder_ref[...]

    @pl.when(step == 0)
    def _():
        offset = pos_ref[0] * atoms
        same = lax.broadcasted_iota(jnp.int32, (devices, edges), 0) == holder
        named = jnp.where(same, 1.0, 0.0)
        named_bf = named.astype(BF16)
        rows = lax.broadcasted_iota(jnp.int32, (CHUNK, CHUNK), 0)
        cols = lax.broadcasted_iota(jnp.int32, (CHUNK, CHUNK), 1)
        earlier = indicator(rows < cols)
        carry = jnp.zeros((devices, 1), F32)
        for c in range(edges // CHUNK):
            part = slice(c * CHUNK, (c + 1) * CHUNK)
            before = matmul(named_bf[:, part], earlier) + carry
            carry = carry + jnp.sum(named[:, part], axis=1, keepdims=True)
            rank_ref[:, part] = jnp.sum(
                before * named[:, part], axis=0, keepdims=True
            ).astype(jnp.int32)
        rank = rank_ref[...]

        def table_of(nodes, spec):
            kinds = jnp.broadcast_to((spec[...] + 1).astype(F32), (TAIL, atoms)).astype(BF16)
            return jnp.concatenate([nodes[...].T, kinds], axis=0)

        table_mid = table_of(node_mid, spec_mid)
        table = jnp.concatenate(
            [table_of(node_lo, spec_lo), table_mid, table_of(node_hi, spec_hi)], axis=1
        )
        channels = node_mid.shape[1]
        ids = lax.broadcasted_iota(jnp.int32, (atoms, edges), 0)
        from_dst = matmul(table_mid, indicator(ids == dst_ref[...] - offset))
        ids = lax.broadcasted_iota(jnp.int32, (3 * atoms, edges), 0)
        from_src = matmul(table, indicator(ids == src_ref[...] - (offset - atoms)))
        xdst = from_dst[:channels].astype(BF16)
        xsrc = from_src[:channels].astype(BF16)
        xdst_ref[...] = xdst
        xsrc_ref[...] = xsrc
        _, first, mixpre = layers(xdst, xsrc, attr_ref, w_dst, w_src, w_attr, w_mix)
        second_ref[...] = (first.astype(F32) + mixpre * jax.nn.sigmoid(mixpre)).astype(BF16)
        tagged = jnp.concatenate(
            [named * from_dst[channels : channels + 1], named * from_src[channels : channels + 1]],
            axis=0,
        ).astype(BF16)
        at_rank = indicator(lax.broadcasted_iota(jnp.int32, (LANES, edges), 0) == rank)
        tags[...] = matmul_nt(tagged, at_rank)

    slot_onehot(onehot, holder, rank_ref[...], step * EDGE_GROUP, capacity)
    moved = matmul_nt(onehot[...], second_ref[...]).astype(BF16)
    line = lax.broadcasted_iota(jnp.int32, (TAIL, LANES), 0)
    for p in range(EDGE_GROUP):
        out_ref[p, :capacity, :] = moved[p * capacity : (p + 1) * capacity]
        tag_dst = tags[pl.ds(step * EDGE_GROUP + p, 1), :]
        tag_src = tags[pl.ds(devices + step * EDGE_GROUP + p, 1), :]
        tail = jnp.where(line == 0, tag_dst, jnp.where(line == 1, tag_src, 0.0))
        out_ref[p, capacity:, :] = tail.astype(BF16)


def prepare_kernel(
    cg_ref,
    wleft_ref,
    wright_ref,
    mask_ref,
    pick_a,
    pick_b,
    pick_dst,
    pick_src,
    cg_out,
    cg_t,
    wlr_out,
    wlr_t,
    pairs_ref,
):
    rows = cg_out.shape[0]
    orb2 = cg_ref.shape[0]

    def pad_rows(array):
        empty = jnp.zeros((rows - orb2, array.shape[1]), F32)
        return jnp.concatenate([array.astype(F32), empty], axis=0)

    tall = pad_rows(cg_ref[...])
    across = jnp.concatenate([tall, jnp.zeros((rows, rows - orb2), F32)], axis=1)
    cg_out[...] = across.astype(BF16)
    cg_t[...] = across.T.astype(BF16)
    both = jnp.concatenate([pad_rows(wleft_ref[...]), pad_rows(wright_ref[...])], axis=0)
    wlr_out[...] = both.astype(BF16)
    wlr_t[...] = both.T.astype(BF16)
    carried = mask_ref[...].astype(F32).astype(BF16)
    dst = matmul_tn(carried, pick_dst[...]).astype(BF16)
    src = matmul_tn(carried, pick_src[...]).astype(BF16)
    pairs_ref[...] = (matmul(pick_a[...], dst) * matmul(pick_b[...], src)).astype(BF16)


def holder_kernel(
    recv_ref,
    target_ref,
    wlr_ref,
    wlr_t,
    cg_ref,
    cg_t,
    pairs_ref,
    place_ref,
    back_ref,
    grad_ref,
    dlr,
):
    step = pl.program_id(0)
    capacity = recv_ref.shape[1] - TAIL
    width = GROUP * capacity
    channels = recv_ref.shape[2]
    rows = cg_ref.shape[0]
    orb2 = target_ref.shape[1]

    @pl.when(step == 0)
    def _():
        grad_ref[...] = jnp.zeros_like(grad_ref)

    second = recv_ref[:, :capacity, :].reshape(width, channels)
    line = lax.broadcasted_iota(jnp.int32, (GROUP * TAIL, width), 0)
    start = place_ref[0:1, :]
    spread = indicator(lax.broadcasted_iota(jnp.int32, (LANES, width), 0) == place_ref[1:2, :])
    tails = recv_ref[:, capacity:, :].reshape(GROUP * TAIL, LANES)
    tags = matmul(tails, spread)
    tag_dst = jnp.sum(jnp.where(line == start, tags, 0.0), axis=0, keepdims=True)
    tag_src = jnp.sum(jnp.where(line == start + 1, tags, 0.0), axis=0, keepdims=True)
    code = jnp.where(tag_dst > 0.5, (tag_dst - 1.0) * KINDS + (tag_src - 1.0), -1.0)
    pair_line = lax.broadcasted_iota(jnp.int32, (pairs_ref.shape[1], width), 0)
    pair = indicator(pair_line == code.astype(jnp.int32))

    both = matmul_nt(wlr_ref[...], second)
    left = both[:rows]
    right = both[rows:]
    predicted = matmul(cg_t[...], (left * right).astype(BF16))
    mask = matmul(pairs_ref[...], pair)
    goal = target_ref[0].astype(F32)
    goal = jnp.concatenate([goal, jnp.zeros((rows - orb2, width), F32)], axis=0)
    resid = mask * (predicted - goal)
    error = jnp.sum(resid * resid, axis=0, keepdims=True) / orb2
    dpred = (resid * (1.0 / orb2)).astype(BF16)
    dcoupled = matmul(cg_ref[...], dpred)
    dlr[:rows] = (dcoupled * right).astype(BF16)
    dlr[rows:] = (dcoupled * left).astype(BF16)
    grad_ref[4 * channels : 4 * channels + 2 * rows] += matmul(dlr[...], second)
    moved = matmul(wlr_t[...], dlr[...]).T.astype(BF16)
    for q in range(GROUP):
        back_ref[q, :capacity, :] = moved[q * capacity : (q + 1) * capacity]
    high = error.astype(BF16).astype(F32)
    middle = (error - high).astype(BF16).astype(F32)
    packed = jnp.where(line == start + 2, error - high - middle, 0.0)
    packed = jnp.where(line == start + 1, middle, packed)
    packed = jnp.where(line == start, high, packed).astype(BF16)
    spelled = matmul_nt(packed, spread).astype(BF16)
    for q in range(GROUP):
        back_ref[q, capacity:, :] = spelled[q * TAIL : (q + 1) * TAIL]


def finish_kernel(
    back_ref,
    holder_ref,
    rank_ref,
    xdst_hbm,
    xsrc_hbm,
    attr_hbm,
    w_dst,
    w_src,
    w_attr,
    w_mix,
    before_ref,
    grad_ref,
    error_ref,
    onehot,
    dsecond,
    found,
    xdst_ref,
    xsrc_ref,
    attr_ref,
    sems,
):
    step = pl.program_id(0)
    capacity = back_ref.shape[1] - TAIL
    edges = holder_ref.shape[1]
    channels = back_ref.shape[2]
    holder = holder_ref[...]
    rank = rank_ref[...]

    wanted = ((xdst_hbm, xdst_ref), (xsrc_hbm, xsrc_ref), (attr_hbm, attr_ref))
    loads = [
        pltpu.make_async_copy(source, kept, sems.at[i])
        for i, (source, kept) in enumerate(wanted)
    ]

    @pl.when(step == 0)
    def _():
        for load in loads:
            load.start()
        dsecond[...] = jnp.zeros_like(dsecond)
        found[...] = jnp.zeros_like(found)

    slot_onehot(onehot, holder, rank, step * EDGE_GROUP, capacity)
    rows = back_ref[:, :capacity, :].reshape(EDGE_GROUP * capacity, channels)
    dsecond[...] += matmul_tn(rows, onehot[...])
    line = lax.broadcasted_iota(jnp.int32, (EDGE_GROUP * TAIL, edges), 0)
    low = (holder - step * EDGE_GROUP) * TAIL
    at_holder = indicator(jnp.logical_and(line >= low, line < low + TAIL))
    tails = back_ref[:, capacity:, :].reshape(EDGE_GROUP * TAIL, LANES)
    found[...] += matmul_tn(tails, at_holder)

    @pl.when(step == pl.num_programs(0) - 1)
    def _():
        for load in loads:
            load.wait()
        place = lax.broadcasted_iota(jnp.int32, found.shape, 0)
        error_ref[...] = jnp.sum(
            jnp.where(place == rank, found[...], 0.0), axis=0, keepdims=True
        )
        dsec = dsecond[...]
        pre, first, mixpre = layers(
            xdst_ref[...], xsrc_ref[...], attr_ref, w_dst, w_src, w_attr, w_mix
        )
        dmix = (dsec * slope(mixpre, jax.nn.sigmoid(mixpre))).astype(BF16)
        dfirst = dsec + matmul(w_mix[...], dmix)
        dpre = (dfirst * slope(pre, jax.nn.sigmoid(pre))).astype(BF16)
        grad_ref[0:channels] = matmul_nt(xdst_ref[...], dpre)
        grad_ref[channels : 2 * channels] = matmul_nt(xsrc_ref[...], dpre)
        grad_ref[2 * channels : 3 * channels] = matmul(dpre, attr_ref[...]).T
        grad_ref[3 * channels : 4 * channels] = matmul_nt(first, dmix)


def exchange(array, axis, groups=None):
    return lax.all_to_all(
        array, axis, split_axis=0, concat_axis=0, tiled=True, axis_index_groups=groups
    )


WIDE, NARROW, DEEP = 4, 4, 8
PEERS = WIDE * NARROW
SWAP = [(i, i ^ 1) for i in range(WIDE * 2)]
PLANE = [
    [(y * 2 + c) * NARROW * DEEP + z * NARROW + x for y in range(WIDE) for x in range(NARROW)]
    for c in range(2)
    for z in range(DEEP)
]
COLUMN = [[z * NARROW + x for z in range(DEEP)] for x in range(NARROW)]


def sum_everywhere(part):
    half = part.shape[0] // 2
    core = lax.rem(lax.axis_index("rep"), 2)
    keep = lax.dynamic_slice_in_dim(part, core * half, half, 0)
    give = lax.dynamic_slice_in_dim(part, (1 - core) * half, half, 0)
    part = keep + lax.ppermute(give, "rep", SWAP)
    got = exchange(part, ("rep", "edge"), PLANE)
    part = jnp.sum(got.reshape(PEERS, half // PEERS, -1), axis=0)
    got = exchange(jnp.tile(part, (DEEP, 1)), "edge", COLUMN)
    part = jnp.sum(got.reshape(DEEP, *part.shape), axis=0)
    part = exchange(jnp.tile(part, (PEERS, 1)), ("rep", "edge"), PLANE)
    other = lax.ppermute(part, "rep", SWAP)
    low = jnp.where(core == 0, part, other)
    high = jnp.where(core == 0, other, part)
    return jnp.concatenate([low, high], axis=0)


def local(
    node_feats,
    edge_attr,
    edge_src,
    edge_dst,
    species,
    orbital_mask,
    tile_owner,
    target_send,
    w_dst,
    w_src,
    w_attr,
    w_mix,
    w_left,
    w_right,
    cg_basis,
):
    atoms, channels = node_feats.shape[1:]
    edges = edge_attr.shape[1]
    orb2, columns = target_send.shape[1:]
    devices = lax.axis_size("edge")
    capacity = columns // devices
    steps = devices // GROUP
    width = GROUP * capacity
    block = capacity + TAIL
    position = lax.axis_index("edge").astype(jnp.int32)[None]
    nodes = node_feats[0]
    node_lo = lax.ppermute(nodes, "edge", ring(devices, 1))
    node_hi = lax.ppermute(nodes, "edge", ring(devices, -1))
    attr = edge_attr[0]
    rows = -(-orb2 // 32) * 32
    holder = tile_owner.reshape(1, edges)
    params = pltpu.CompilerParams(vmem_limit_bytes=VMEM)

    def whole(shape):
        return pl.BlockSpec(shape, lambda *_: (0,) * len(shape))

    def array(shape, dtype=BF16):
        return jax.ShapeDtypeStruct(shape, dtype)

    square = whole((channels, channels))
    line = whole((1, edges))
    packets = pl.BlockSpec((GROUP, block, channels), lambda i, *_: (i, 0, 0))
    edge_packets = pl.BlockSpec((EDGE_GROUP, block, channels), lambda i, *_: (i, 0, 0))

    wide = whole((channels, edges))
    edge_steps = devices // EDGE_GROUP
    onehot = pltpu.VMEM((EDGE_GROUP * capacity, edges), BF16)

    def kinds_of(shift):
        return pl.BlockSpec(
            (1, atoms), lambda i, pos: (0, jnp.clip(pos[0] + shift, 0, devices - 1))
        )

    sent, rank, xdst, xsrc = pl.pallas_call(
        edge_kernel,
        out_shape=(
            array((devices, block, channels)),
            array((1, edges), jnp.int32),
            array((channels, edges)),
            array((channels, edges)),
        ),
        grid_spec=pltpu.PrefetchScalarGridSpec(
            num_scalar_prefetch=1,
            grid=(edge_steps,),
            in_specs=[line, line, line, kinds_of(-1), kinds_of(0), kinds_of(1)]
            + [whole((atoms, channels))] * 3
            + [whole((edges, channels))]
            + [square] * 4,
            out_specs=[edge_packets, line] + [wide] * 2,
            scratch_shapes=[
                pltpu.VMEM((channels, edges), BF16),
                onehot,
                pltpu.VMEM((2 * devices, LANES), F32),
            ],
        ),
        compiler_params=params,
    )(
        position,
        edge_dst,
        edge_src,
        holder,
        species,
        species,
        species,
        node_lo,
        nodes,
        node_hi,
        attr,
        w_dst,
        w_src,
        w_attr,
        w_mix,
    )
    received = exchange(sent, "edge")

    species_count, orbs = orbital_mask.shape
    entry = np.arange(rows)[:, None]
    orbit = np.arange(orbs)[None, :]
    valid = entry < orb2
    pick_a = (valid & (entry // orbs == orbit)).astype(BF16)
    pick_b = (valid & (entry % orbs == orbit)).astype(BF16)
    code = np.arange(TAIL)[None, :]
    kind = np.arange(species_count)[:, None]
    known = code < species_count**2
    pick_dst = (known & (code // species_count == kind)).astype(BF16)
    pick_src = (known & (code % species_count == kind)).astype(BF16)
    prepared = [
        array((rows, rows)),
        array((rows, rows)),
        array((2 * rows, channels)),
        array((channels, 2 * rows)),
        array((rows, TAIL)),
    ]
    ready = pl.pallas_call(prepare_kernel, out_shape=prepared, compiler_params=pltpu.CompilerParams(vmem_limit_bytes=24 << 20))(
        cg_basis, w_left, w_right, orbital_mask, pick_a, pick_b, pick_dst, pick_src
    )
    cg, cg_t, wlr, wlr_t, pairs = ready

    slots = np.arange(width)
    places = np.stack([slots // capacity * TAIL, slots % capacity]).astype(np.int32)
    unit = 2 * PEERS * 8
    total = -(-(4 * channels + 2 * rows) // unit) * unit
    shared = (wlr, wlr_t, cg, cg_t, pairs, places)
    back, grads = pl.pallas_call(
        holder_kernel,
        out_shape=(array((devices, block, channels)), array((total, channels), F32)),
        grid=(steps,),
        in_specs=[
            packets,
            pl.BlockSpec((1, orb2, width), lambda i: (0, 0, i)),
            *[whole(a.shape) for a in shared],
        ],
        out_specs=[packets, whole((total, channels))],
        scratch_shapes=[pltpu.VMEM((2 * rows, width), BF16)],
        compiler_params=pltpu.CompilerParams(vmem_limit_bytes=52 << 20),
    )(received, target_send, *shared)
    returned = exchange(back, "edge")

    grads, errors = pl.pallas_call(
        finish_kernel,
        out_shape=(array((total, channels), F32), array((1, edges), F32)),
        grid=(edge_steps,),
        in_specs=[edge_packets, line, line]
        + [pl.BlockSpec(memory_space=pl.ANY)] * 3
        + [square] * 4
        + [pl.BlockSpec(memory_space=pl.ANY)],
        out_specs=[whole((4 * channels, channels)), line],
        scratch_shapes=[
            onehot,
            pltpu.VMEM((channels, edges), F32),
            pltpu.VMEM((LANES, edges), F32),
            pltpu.VMEM((channels, edges), BF16),
            pltpu.VMEM((channels, edges), BF16),
            pltpu.VMEM((edges, channels), BF16),
            pltpu.SemaphoreType.DMA((3,)),
        ],
        input_output_aliases={10: 0},
        compiler_params=params,
    )(returned, holder, rank, xdst, xsrc, attr, w_dst, w_src, w_attr, w_mix, grads)

    grads = sum_everywhere(grads)
    outs = [grads[i * channels : (i + 1) * channels] for i in range(4)]
    outs += [grads[4 * channels + i * rows :][:orb2] for i in range(2)]
    return (*outs, errors)


def solution(mesh):
    return jax.shard_map(
        local,
        mesh=mesh,
        in_specs=(
            P("rep", "edge", None),
            P("rep", "edge", None),
            P("rep", "edge"),
            P("rep", "edge"),
            P("rep", None),
            P(),
            P("rep", "edge", None),
            P("rep", "edge", None),
            P(),
            P(),
            P(),
            P(),
            P(),
            P(),
            P(),
        ),
        out_specs=(P(), P(), P(), P(), P(), P(), P("rep", "edge")),
        check_vma=False,
    )
```
